256 devices in a mesh: section: 8 (over y_lo, x), ep: 32 (over y_hi, z, core).
Axes of the slice: x: 4, y: 4 (y_hi: 2, y_lo: 2; y = y_hi * 2 + y_lo), z: 8, core: 2. Of those that a mesh axis runs over, the one named last changes fastest.
Arguments:
- act_fwd: bfloat16 [8, 512, 7168], P('section', 'ep'), may hold values from -6 to 6
- act_saved: bfloat16 [8, 512, 7168], P('section', 'ep'), may hold values from -6 to 6
- cot_in: bfloat16 [8, 512, 7168], P('section', 'ep'), may hold values from -6 to 6
- routes_fwd: int32 [8, 512, 2], P('section', 'ep'), may hold values from 0 to 7, all different within a row; in each aligned block of 16 rows (0 to 15, 16 to 31, ..., all dimensions but the last counted through in order) at most 6 rows name the same one
- routes_bwd: int32 [8, 512, 2], P('section', 'ep'), may hold values from 0 to 7, all different within a row; in each aligned block of 16 rows (0 to 15, 16 to 31, ..., all dimensions but the last counted through in order) at most 6 rows name the same one
- w_gate: bfloat16 [8, 7168, 8192], P('section', None, 'ep'), may hold values from -0.0625 to 0.0625
- w_up: bfloat16 [8, 7168, 8192], P('section', None, 'ep'), may hold values from -0.0625 to 0.0625
- w_down: bfloat16 [8, 8192, 7168], P('section', 'ep'), may hold values from -0.1875 to 0.1875
- router: float32 [8, 7168, 8], P('section'), may hold values from -0.0625 to 0.0625
- norm_gain: float32 [8, 7168], P('section'), may hold values from 0.1 to 1.9
Outputs:
- fwd_next: bfloat16 [8, 512, 7168], P('section', 'ep')
- cot_next: bfloat16 [8, 512, 7168], P('section', 'ep')
The draws below stay inside these ranges and needn't reach their ends.
Inputs may be any that keep to these rules, and one draw needn't show every extreme that they name: `routes_fwd`: among the 16 tokens of one device (aligned blocks of 16 rows of a section), no expert is named by more than 6 tokens, and in some block one expert is named by exactly 6; every expert is named somewhere; a token's 2 experts differ. `routes_bwd`: as for routes_fwd.
All inputs are finite; a program needn't handle non-finite values.
Results may differ from the reference program's by a relative error of at most 0.008.
Values may be sent and summed in bfloat16 or wider, within the bound.
No kernel may reach another device: no remote copies, remote signals or barrier semaphores. Data moves between devices by JAX's collectives and lax.ppermute only.
A program may use at most 128 MiB of HBM per device.

```python
import math
import jax
import jax.numpy as jnp
import numpy as np
from jax import lax

D = 7168
FFE = 1024
EXPERTS = 8
TOPK = 2
TOK_DEV = 16
CAP = 6
GROUP = 4
FF_DEV = 256
TOKENS = 512
SECTIONS = 8
N_EP = 32


def block_levels(stream_key, shape, cuts, least, top_value):
    def one(dim, parts):
        steps = jax.random.uniform(jax.random.fold_in(jax.random.fold_in(stream_key, 6), dim), (parts,), jnp.float32, least / len(cuts), top_value / len(cuts))
        return jnp.repeat(jnp.exp(steps), shape[dim] // parts).reshape((-1,) + (1,) * (len(shape) - dim - 1))

    loudness = one(*cuts[0])
    for cut in cuts[1:]:
        loudness = loudness * one(*cut)
    return loudness


def deal_out(stream_key, own, number, rows, count, top, most, lean):
    order = jax.random.permutation(stream_key, count)
    crowded, usual = portions_of(count, rows * top, most, lean, True), portions_of(count, rows * top, most, lean, False)
    places = jnp.arange(count)

    def named(lengths, rotation):
        used = int((lengths > 0).sum())
        fixed = max(1, used // 4)
        moved = fixed + (places - fixed + rotation * (used - fixed)) % max(1, count - fixed)
        return jnp.zeros((count,), jnp.int32).at[order[jnp.where(places < fixed, places, moved)]].set(jnp.asarray(lengths, jnp.int32))

    lengths = jnp.where(number % 4 == 0, named(crowded, number // 4), named(usual, number - number // 4 - 1))
    mixed = jax.random.permutation(jax.random.fold_in(own, 3), count)
    source_of, sink = mixed[0:count // 2 * 2:2], mixed[1:count // 2 * 2:2]
    room = jnp.minimum(lengths[source_of] - 1, most - lengths[sink]) // 2
    room = jnp.where((source_of == order[0]) | (sink == order[0]) | (lengths[sink] == 0), 0, jnp.maximum(room, 0))
    moved = jax.random.randint(jax.random.fold_in(own, 4), (count // 2,), 0, 1 << 20) % (room + 1)
    lengths = lengths.at[source_of].add(-moved).at[sink].add(moved)
    labels = jnp.searchsorted(jnp.cumsum(lengths), jnp.arange(rows * top), side="right").astype(jnp.int32)
    listing = labels.reshape(top, rows).T
    listing = listing[jax.random.permutation(jax.random.fold_in(own, 1), rows)]
    rotation = jax.random.randint(jax.random.fold_in(own, 2), (rows, 1), 0, top)
    return jnp.take_along_axis(listing, (jnp.arange(top)[None, :] + rotation) % top, axis=1)


def portions_of(number_of, total, bound, slope, full):
    loads = [(1 << 20) // math.isqrt(rank ** slope) + 1 for rank in range(1, number_of + 1)]
    largest = bound if full else min(bound, max(-(-total // number_of), total * loads[0] // sum(loads)))
    least = 1 if total - largest >= number_of - 1 else 0
    counts, surplus = [largest] + [least] * (number_of - 1), total - largest - least * (number_of - 1)
    while surplus > 0:
        candidates = [i for i in range(1, number_of) if counts[i] < largest] or [i for i in range(1, number_of) if counts[i] < bound]
        mass, left = sum([loads[i] for i in candidates]), surplus
        for i in candidates:
            more = min(bound - counts[i], max(1, left * loads[i] // mass), surplus)
            counts[i] = counts[i] + more
            surplus = surplus - more
    return np.array(counts)


def normal_values(rng, shape, deviation, bound, shards=(), kind=jnp.bfloat16):
    factor_of = block_levels(rng, shape, shards, -0.22, 0.18) if shards else 1.0
    drawn = jax.random.normal(rng, shape, jnp.float32) * deviation * factor_of
    return jnp.minimum(jnp.maximum(drawn, -bound), bound).astype(kind)


def setup_inputs(seed: int = 0) -> dict:
    splits = jax.random.split(jax.random.key(seed), 11)
    act_fwd = normal_values(splits[0], (SECTIONS, TOKENS, D), 1.0, 6.0, ((0, 8), (1, 32)))
    act_saved = normal_values(splits[1], (SECTIONS, TOKENS, D), 1.0, 6.0, ((0, 8), (1, 32)))
    cot_in = normal_values(splits[2], (SECTIONS, TOKENS, D), 1.0, 6.0, ((0, 8), (1, 32)))
    routes_fwd_keys = jax.random.split(jax.random.fold_in(splits[3], 1), SECTIONS * TOKENS // TOK_DEV)
    routes_fwd_turns = jax.random.permutation(jax.random.fold_in(splits[3], 3), SECTIONS * TOKENS // TOK_DEV)
    routes_fwd = jax.vmap(lambda own, number: deal_out(jax.random.fold_in(splits[3], 2), own, number, TOK_DEV, EXPERTS, TOPK, CAP, 2))(routes_fwd_keys, routes_fwd_turns).reshape((SECTIONS, TOKENS, TOPK))
    routes_bwd_keys = jax.random.split(jax.random.fold_in(splits[4], 1), SECTIONS * TOKENS // TOK_DEV)
    routes_bwd_turns = jax.random.permutation(jax.random.fold_in(splits[4], 3), SECTIONS * TOKENS // TOK_DEV)
    routes_bwd = jax.vmap(lambda own, number: deal_out(jax.random.fold_in(splits[4], 2), own, number, TOK_DEV, EXPERTS, TOPK, CAP, 2))(routes_bwd_keys, routes_bwd_turns).reshape((SECTIONS, TOKENS, TOPK))
    w_gate = normal_values(splits[5], (SECTIONS, D, EXPERTS * FFE), D ** -0.5, 0.0625, ((0, 8), (2, 32)))
    w_up = normal_values(splits[6], (SECTIONS, D, EXPERTS * FFE), D ** -0.5, 0.0625, ((0, 8), (2, 32)))
    w_down = normal_values(splits[7], (SECTIONS, EXPERTS * FFE, D), FFE ** -0.5, 0.1875, ((0, 8), (1, 32)))
    router = normal_values(splits[8], (SECTIONS, D, EXPERTS), D ** -0.5, 0.0625, ((0, 8),), jnp.float32)
    norm_gain = jnp.clip(1.0 + 0.18 * jax.random.normal(splits[9], (SECTIONS, D), jnp.float32), 0.1, 1.9)
    return dict(act_fwd=act_fwd, act_saved=act_saved, cot_in=cot_in, routes_fwd=routes_fwd, routes_bwd=routes_bwd, w_gate=w_gate, w_up=w_up, w_down=w_down, router=router, norm_gain=norm_gain)


routed_scale = 2.5

def rounded(values):
    return lax.optimization_barrier(values.astype(jnp.bfloat16))

def normalize(activations, gain):
    widened = activations.astype(jnp.float32)
    inverse = lax.rsqrt(lax.optimization_barrier(jnp.mean(widened * widened, axis=-1, keepdims=True)) + 1e-06)
    return ((widened * inverse * gain).astype(jnp.bfloat16), inverse)

def gate_values(normed, table, expert_ids):
    logits = jnp.dot(normed.astype(jnp.float32), table, precision=lax.Precision.HIGHEST)
    affinity = jax.nn.sigmoid(logits)
    onehot = (expert_ids[:, :, None] == jnp.arange(EXPERTS, dtype=jnp.int32)[None, None, :]).astype(jnp.float32)
    chosen = lax.optimization_barrier(jnp.sum(onehot * affinity[:, None, :], axis=-1))
    summed = lax.optimization_barrier(jnp.sum(chosen, axis=-1, keepdims=True))
    return (routed_scale * chosen / summed, chosen, summed, onehot)

def buffer_positions(expert_ids):
    flat_ids = expert_ids.reshape(N_EP, TOK_DEV * TOPK)
    onehot = (flat_ids[:, :, None] == jnp.arange(EXPERTS, dtype=jnp.int32)[None, None, :]).astype(jnp.int32)
    running = jnp.cumsum(onehot, axis=1)
    slot_ids = lax.optimization_barrier(jnp.sum(onehot * (running - 1), axis=-1))
    source = jnp.arange(N_EP, dtype=jnp.int32)[:, None]
    return ((flat_ids * N_EP + source) * CAP + slot_ids).reshape(TOKENS * TOPK).astype(jnp.int32)

def expert_forward(packed, gate_cols, up_cols, down_rows):
    accum = jnp.zeros((packed.shape[0], D), jnp.float32)
    for block in range(GROUP):
        first = block * FF_DEV
        gate_proj = jnp.dot(packed, gate_cols[:, first:first + FF_DEV], preferred_element_type=jnp.float32)
        up_proj = jnp.dot(packed, up_cols[:, first:first + FF_DEV], preferred_element_type=jnp.float32)
        hidden = rounded(jax.nn.silu(gate_proj) * up_proj)
        part_out = rounded(jnp.dot(hidden, down_rows[first:first + FF_DEV], preferred_element_type=jnp.float32))
        accum = accum + part_out.astype(jnp.float32)
    return accum

def expert_backward(packed, grads, gate_cols, up_cols, down_rows):
    accum = jnp.zeros((packed.shape[0], D), jnp.float32)
    dot_accum = jnp.zeros((packed.shape[0],), jnp.float32)
    dims = (((1,), (1,)), ((), ()))
    for block in range(GROUP):
        first = block * FF_DEV
        gate_part = gate_cols[:, first:first + FF_DEV]
        up_part = up_cols[:, first:first + FF_DEV]
        down_part = down_rows[first:first + FF_DEV]
        gate_proj = jnp.dot(packed, gate_part, preferred_element_type=jnp.float32)
        up_proj = jnp.dot(packed, up_part, preferred_element_type=jnp.float32)
        sigmoid_gate = jax.nn.sigmoid(gate_proj)
        activated = gate_proj * sigmoid_gate
        hidden = rounded(activated * up_proj)
        part_out = rounded(jnp.dot(hidden, down_part, preferred_element_type=jnp.float32))
        dots = rounded(lax.optimization_barrier(jnp.sum(part_out.astype(jnp.float32) * grads.astype(jnp.float32), axis=-1)))
        dot_accum = dot_accum + dots.astype(jnp.float32)
        grad_hidden = lax.dot_general(grads, down_part, dims, preferred_element_type=jnp.float32)
        grad_gate = rounded(grad_hidden * up_proj * sigmoid_gate * (1.0 + gate_proj * (1.0 - sigmoid_gate)))
        grad_up = rounded(grad_hidden * activated)
        grad_rows = lax.dot_general(grad_gate, gate_part, dims, preferred_element_type=jnp.float32)
        grad_rows = grad_rows + lax.dot_general(grad_up, up_part, dims, preferred_element_type=jnp.float32)
        accum = accum + rounded(grad_rows).astype(jnp.float32)
    return (accum, dot_accum)

def one_section(pack):
    fwd_rows, saved_rows, grad_rows, ids_fwd, ids_bwd, gate_w, up_w, down_w, table, gain = pack
    gate_exp = gate_w.reshape(D, EXPERTS, FFE).transpose(1, 0, 2)
    up_exp = up_w.reshape(D, EXPERTS, FFE).transpose(1, 0, 2)
    down_exp = down_w.reshape(EXPERTS, FFE, D)
    slots_all = N_EP * CAP
    normed, inverse = normalize(fwd_rows, gain)
    weights = gate_values(normed, table, ids_fwd)[0]
    position = buffer_positions(ids_fwd)
    packed = jnp.zeros((EXPERTS * slots_all, D), jnp.bfloat16).at[position].set(jnp.repeat(normed, TOPK, axis=0))

    def run_forward(item):
        return expert_forward(item[0], item[1], item[2], item[3])
    produced = lax.map(run_forward, (packed.reshape(EXPERTS, slots_all, D), gate_exp, up_exp, down_exp))
    expert_out = produced.reshape(EXPERTS * slots_all, D)[position].reshape(TOKENS, TOPK, D)
    result_fwd = (fwd_rows.astype(jnp.float32) + lax.optimization_barrier(jnp.sum(weights[:, :, None] * expert_out, axis=1))).astype(jnp.bfloat16)
    normed_bwd, inverse_bwd = normalize(saved_rows, gain)
    weights_bwd, chosen, summed, onehot = gate_values(normed_bwd, table, ids_bwd)
    position_bwd = buffer_positions(ids_bwd)
    packed_bwd = jnp.zeros((EXPERTS * slots_all, D), jnp.bfloat16).at[position_bwd].set(jnp.repeat(normed_bwd, TOPK, axis=0))
    packed_grad = jnp.zeros((EXPERTS * slots_all, D), jnp.bfloat16).at[position_bwd].set(jnp.repeat(grad_rows, TOPK, axis=0))

    def run_backward(item):
        return expert_backward(item[0], item[1], item[2], item[3], item[4])
    grad_back, dot_back = lax.map(run_backward, (packed_bwd.reshape(EXPERTS, slots_all, D), packed_grad.reshape(EXPERTS, slots_all, D), gate_exp, up_exp, down_exp))
    grad_assign = grad_back.reshape(EXPERTS * slots_all, D)[position_bwd].reshape(TOKENS, TOPK, D)
    dot_assign = dot_back.reshape(EXPERTS * slots_all)[position_bwd].reshape(TOKENS, TOPK)
    grad_normed = lax.optimization_barrier(jnp.sum(weights_bwd[:, :, None] * grad_assign, axis=1))
    cross = lax.optimization_barrier(jnp.sum(dot_assign * chosen, axis=-1, keepdims=True))
    grad_aff = routed_scale * (dot_assign / summed - cross / (summed * summed))
    grad_logit = grad_aff * chosen * (1.0 - chosen)
    grad_table = lax.optimization_barrier(jnp.sum(onehot * grad_logit[:, :, None], axis=1))
    grad_normed = grad_normed + lax.dot_general(grad_table, table, (((1,), (1,)), ((), ())), precision=lax.Precision.HIGHEST)
    scaled = gain * grad_normed
    widened = saved_rows.astype(jnp.float32)
    grad_input = inverse_bwd * scaled - widened * inverse_bwd * inverse_bwd * inverse_bwd * lax.optimization_barrier(jnp.mean(widened * scaled, axis=-1, keepdims=True))
    result_bwd = (grad_rows.astype(jnp.float32) + grad_input).astype(jnp.bfloat16)
    return (result_fwd, result_bwd)

def reference(act_fwd, act_saved, cot_in, routes_fwd, routes_bwd, w_gate, w_up, w_down, router, norm_gain):
    outputs_fwd, outputs_bwd = lax.map(one_section, (act_fwd, act_saved, cot_in, routes_fwd, routes_bwd, w_gate, w_up, w_down, router, norm_gain))
    return (jnp.roll(outputs_fwd, 1, axis=0), jnp.roll(outputs_bwd, -1, axis=0))
```

```python
import jax
import jax.numpy as jnp
from jax import lax
from jax.sharding import PartitionSpec as P

EXPERTS = 8
TOPK = 2
CAP = 6
PAIRS = 4
SLOTS = EXPERTS * CAP

routed_scale = 2.5


def place_of(index):
    return index // 16, index // 2 % 8, index % 2


def route_of(step):
    def target(index):
        y, z, core = place_of(index)
        sign = -1 if z % 2 else 1
        y, z, core = step(y, z, core, sign)
        return y * 16 + z % 8 * 2 + core

    return [(i, target(i)) for i in range(32)]


def back_of(route):
    return [(b, a) for a, b in route]


SWAP_Y = route_of(lambda y, z, core, sign: (1 - y, z, core))
SWAP_CORE = route_of(lambda y, z, core, sign: (y, z, 1 - core))
SWAP_PAIR = route_of(lambda y, z, core, sign: (y, z + sign, core))
ENTER = {
    1: route_of(lambda y, z, core, sign: (y, z + 2 * sign, core)),
    2: route_of(lambda y, z, core, sign: (y, z - 3 * sign, core)),
    3: route_of(lambda y, z, core, sign: (y, z - sign, core)),
}


def send(block, route):
    return lax.ppermute(block, "ep", route)


def from_behind(block, axis, distance):
    devices = range(lax.axis_size(axis))
    route = [((i - distance) % len(devices), i) for i in devices]
    return lax.ppermute(block, axis, route)


def normalize(activations, gain):
    widened = activations.astype(jnp.float32)
    inverse = lax.rsqrt(jnp.mean(widened * widened, axis=-1, keepdims=True) + 1e-06)
    return ((widened * inverse * gain).astype(jnp.bfloat16), inverse)


def gate_values(normed, table, expert_ids):
    logits = jnp.dot(normed.astype(jnp.float32), table, precision=lax.Precision.HIGHEST)
    affinity = jax.nn.sigmoid(logits)
    onehot = (
        expert_ids[:, :, None] == jnp.arange(table.shape[1], dtype=jnp.int32)[None, None, :]
    ).astype(jnp.float32)
    chosen = jnp.sum(onehot * affinity[:, None, :], axis=-1)
    summed = jnp.sum(chosen, axis=-1, keepdims=True)
    return (routed_scale * chosen / summed, chosen, summed, onehot)


def slots_of(expert_ids):
    y, z, _ = place_of(lax.axis_index("ep"))
    flat_ids = expert_ids.reshape(-1)
    onehot = (flat_ids[:, None] == jnp.arange(EXPERTS, dtype=jnp.int32)[None, :]).astype(jnp.int32)
    running = jnp.cumsum(onehot, axis=0)
    slot_ids = jnp.sum(onehot * (running - 1), axis=1)
    away = (flat_ids % PAIRS - z // 2) % PAIRS
    role = jnp.where(z % 2 == 1, (PAIRS - away) % PAIRS, away)
    other = jnp.where(flat_ids // PAIRS == y, 0, PAIRS)
    target = (other + role) * CAP + slot_ids
    slots = (target[:, None] == jnp.arange(SLOTS, dtype=jnp.int32)[None, :]).astype(jnp.float32)
    return slots.reshape(expert_ids.shape + (SLOTS,))


def pack_rows(slots, token_rows):
    placer = jnp.sum(slots, axis=1).astype(jnp.bfloat16)
    return lax.dot_general(
        placer, token_rows, (((0,), (0,)), ((), ())), preferred_element_type=jnp.float32
    ).astype(jnp.bfloat16)


def dispatch(packed):
    half = SLOTS // 2
    here = packed.reshape(2, PAIRS, CAP, -1)
    both = jnp.stack([here[0], send(here[1], SWAP_Y)], axis=1)
    mine = jnp.concatenate(
        [both[0].reshape(2 * CAP, -1)]
        + [send(both[r].reshape(2 * CAP, -1), ENTER[r]) for r in (1, 2, 3)]
    )
    chip = jnp.concatenate([mine, send(mine, SWAP_PAIR)])
    return jnp.concatenate([chip, send(chip, SWAP_CORE)])


def add(a, b):
    return (a.astype(jnp.float32) + b.astype(jnp.float32)).astype(jnp.bfloat16)


def give_back(parts):
    chip = add(parts[: 2 * SLOTS], send(parts[2 * SLOTS :], SWAP_CORE))
    mine = add(chip[:SLOTS], send(chip[SLOTS:], SWAP_PAIR))
    mine = mine.reshape(PAIRS, 2 * CAP, -1)
    both = [mine[0]] + [send(mine[r], back_of(ENTER[r])) for r in (1, 2, 3)]
    both = jnp.stack(both).reshape(PAIRS, 2, CAP, -1)
    here, there = both[:, 0], both[:, 1]
    return jnp.concatenate([here, send(there, SWAP_Y)]).reshape(SLOTS, -1)


def expert_forward(rows, gate_cols, up_cols, down_rows):
    gate_proj = jnp.dot(rows, gate_cols, preferred_element_type=jnp.float32)
    up_proj = jnp.dot(rows, up_cols, preferred_element_type=jnp.float32)
    hidden = (jax.nn.silu(gate_proj) * up_proj).astype(jnp.bfloat16)
    return jnp.dot(hidden, down_rows, preferred_element_type=jnp.float32).astype(jnp.bfloat16)


def expert_backward(rows, grads, gate_cols, up_cols, down_rows):
    dims = (((1,), (1,)), ((), ()))
    gate_proj = jnp.dot(rows, gate_cols, preferred_element_type=jnp.float32)
    up_proj = jnp.dot(rows, up_cols, preferred_element_type=jnp.float32)
    sigmoid_gate = jax.nn.sigmoid(gate_proj)
    activated = gate_proj * sigmoid_gate
    hidden = (activated * up_proj).astype(jnp.bfloat16)
    grad_hidden = lax.dot_general(grads, down_rows, dims, preferred_element_type=jnp.float32)
    dots = jnp.sum(hidden.astype(jnp.float32) * grad_hidden, axis=-1)
    grad_gate = (
        grad_hidden * up_proj * sigmoid_gate * (1.0 + gate_proj * (1.0 - sigmoid_gate))
    ).astype(jnp.bfloat16)
    grad_up = (grad_hidden * activated).astype(jnp.bfloat16)
    grad_rows = lax.dot_general(grad_gate, gate_cols, dims, preferred_element_type=jnp.float32)
    grad_rows = grad_rows + lax.dot_general(
        grad_up, up_cols, dims, preferred_element_type=jnp.float32
    )
    column = lax.axis_index("ep") % 4
    lanes = jnp.where(jnp.arange(128)[None, :] == column, dots[:, None], 0.0)
    return jnp.concatenate([grad_rows, lanes], axis=1).astype(jnp.bfloat16)


def local(
    act_fwd, act_saved, cot_in, routes_fwd, routes_bwd, w_gate, w_up, w_down, router, norm_gain
):
    gate_cols = w_gate[0]
    up_cols = w_up[0]
    down_rows = w_down[0]
    table = router[0]
    gain = norm_gain[0]
    fwd_rows = act_fwd[0]
    saved_rows = act_saved[0]
    grad_in = cot_in[0]
    width = fwd_rows.shape[1]

    slots_bwd = slots_of(routes_bwd[0])
    slots_fwd = slots_of(routes_fwd[0])
    arrived_grad = dispatch(pack_rows(slots_bwd, grad_in))
    normed_bwd, inverse_bwd = normalize(saved_rows, gain)
    arrived_bwd = dispatch(pack_rows(slots_bwd, normed_bwd))
    normed_fwd, _ = normalize(fwd_rows, gain)
    arrived_fwd = dispatch(pack_rows(slots_fwd, normed_fwd))
    weights_bwd, chosen, summed, onehot = gate_values(normed_bwd, table, routes_bwd[0])
    weights_fwd = gate_values(normed_fwd, table, routes_fwd[0])[0]

    back_bwd = give_back(expert_backward(arrived_bwd, arrived_grad, gate_cols, up_cols, down_rows))
    back_fwd = give_back(expert_forward(arrived_fwd, gate_cols, up_cols, down_rows))

    mixer_bwd = jnp.sum(weights_bwd[:, :, None] * slots_bwd, axis=1)
    mixer_fwd = jnp.sum(weights_fwd[:, :, None] * slots_fwd, axis=1)

    dot_rows = jnp.sum(back_bwd[:, width:].astype(jnp.float32), axis=-1)
    dot_assign = jnp.sum(slots_bwd * dot_rows, axis=-1)
    grad_normed = jnp.dot(
        mixer_bwd, back_bwd[:, :width].astype(jnp.float32), precision=lax.Precision.HIGHEST
    )
    cross = jnp.sum(dot_assign * chosen, axis=-1, keepdims=True)
    grad_aff = routed_scale * (dot_assign / summed - cross / (summed * summed))
    grad_logit = grad_aff * chosen * (1.0 - chosen)
    grad_table = jnp.sum(onehot * grad_logit[:, :, None], axis=1)
    grad_normed = grad_normed + lax.dot_general(
        grad_table, table, (((1,), (1,)), ((), ())), precision=lax.Precision.HIGHEST
    )
    scaled = gain * grad_normed
    widened = saved_rows.astype(jnp.float32)
    grad_input = (
        inverse_bwd * scaled
        - widened
        * inverse_bwd
        * inverse_bwd
        * inverse_bwd
        * jnp.mean(widened * scaled, axis=-1, keepdims=True)
    )
    result_bwd = (grad_in.astype(jnp.float32) + grad_input).astype(jnp.bfloat16)
    cot_next = from_behind(result_bwd[None], "section", -1)

    expert_out = jnp.dot(
        mixer_fwd, back_fwd.astype(jnp.float32), precision=lax.Precision.HIGHEST
    )
    result_fwd = (fwd_rows.astype(jnp.float32) + expert_out).astype(jnp.bfloat16)
    fwd_next = from_behind(result_fwd[None], "section", 1)
    return (fwd_next, cot_next)


def solution(mesh):
    return jax.shard_map(
        local,
        mesh=mesh,
        in_specs=(
            P("section", "ep", None),
            P("section", "ep", None),
            P("section", "ep", None),
            P("section", "ep", None),
            P("section", "ep", None),
            P("section", None, "ep"),
            P("section", None, "ep"),
            P("section", "ep", None),
            P("section", None, None),
            P("section", None),
        ),
        out_specs=(P("section", "ep", None), P("section", "ep", None)),
        check_vma=False,
    )
```

```python
import jax
import jax.numpy as jnp
import numpy as np
from jax import lax
from jax.sharding import PartitionSpec as P

EXPERTS = 8
TOPK = 2
CAP = 6
PAIRS = 4
SLOTS = EXPERTS * CAP
QUARTERS = 4

routed_scale = 2.5


def place_of(index):
    return index // 16, index // 2 % 8, index % 2


def route_of(step):
    def target(index):
        y, z, core = place_of(index)
        sign = -1 if z % 2 else 1
        y, z, core = step(y, z, core, sign)
        return y * 16 + z % 8 * 2 + core

    return [(i, target(i)) for i in range(32)]


def back_of(route):
    return [(b, a) for a, b in route]


SWAP_Y = route_of(lambda y, z, core, sign: (1 - y, z, core))
SWAP_CORE = route_of(lambda y, z, core, sign: (y, z, 1 - core))
SWAP_PAIR = route_of(lambda y, z, core, sign: (y, z + sign, core))
ENTER = {
    1: route_of(lambda y, z, core, sign: (y, z + 2 * sign, core)),
    2: route_of(lambda y, z, core, sign: (y, z - 3 * sign, core)),
    3: route_of(lambda y, z, core, sign: (y, z - sign, core)),
}


def send(block, route):
    return lax.ppermute(block, "ep", route)


def from_behind(block, axis, distance):
    devices = range(lax.axis_size(axis))
    route = [((i - distance) % len(devices), i) for i in devices]
    return lax.ppermute(block, axis, route)


def normalize(activations, gain):
    widened = activations.astype(jnp.float32)
    inverse = lax.rsqrt(jnp.mean(widened * widened, axis=-1, keepdims=True) + 1e-06)
    return ((widened * inverse * gain).astype(jnp.bfloat16), inverse)


def gate_values(normed, table, expert_ids):
    logits = jnp.dot(normed.astype(jnp.float32), table, precision=lax.Precision.HIGHEST)
    affinity = jax.nn.sigmoid(logits)
    onehot = (
        expert_ids[:, :, None] == jnp.arange(table.shape[1], dtype=jnp.int32)[None, None, :]
    ).astype(jnp.float32)
    chosen = jnp.sum(onehot * affinity[:, None, :], axis=-1)
    summed = jnp.sum(chosen, axis=-1, keepdims=True)
    return (routed_scale * chosen / summed, chosen, summed, onehot)


def slots_of(expert_ids):
    y, z, _ = place_of(lax.axis_index("ep"))
    flat_ids = expert_ids.reshape(-1)
    count = jnp.arange(flat_ids.shape[0], dtype=jnp.int32)
    earlier = (flat_ids[:, None] == flat_ids[None, :]) & (count[None, :] < count[:, None])
    slot_ids = jnp.sum(earlier.astype(jnp.int32), axis=1)
    away = (flat_ids % PAIRS - z // 2) % PAIRS
    role = jnp.where(z % 2 == 1, (PAIRS - away) % PAIRS, away)
    other = jnp.where(flat_ids // PAIRS == y, 0, PAIRS)
    return ((other + role) * CAP + slot_ids).reshape(expert_ids.shape)


def quarter_rows(rows):
    return jnp.concatenate(jnp.split(rows, QUARTERS, axis=1))


def whole_rows(quarters):
    return jnp.concatenate(jnp.split(quarters, QUARTERS), axis=1)


def placing(slots, values):
    unit = QUARTERS * CAP
    row = jnp.arange(QUARTERS * SLOTS, dtype=jnp.int32)[:, None]
    quarter, slot = row % unit // CAP, row // unit * CAP + row % CAP
    column = jnp.arange(QUARTERS * slots.shape[0], dtype=jnp.int32)[None, :]
    same = quarter == column // slots.shape[0]
    placed = 0.0
    for k in range(TOPK):
        hit = same & (slot == jnp.tile(slots[:, k], QUARTERS)[None, :])
        placed = placed + jnp.where(hit, jnp.tile(values[:, k], QUARTERS)[None, :], 0.0)
    return placed


def pack_rows(placer, token_rows):
    return jnp.dot(placer, quarter_rows(token_rows), preferred_element_type=jnp.float32).astype(
        jnp.bfloat16
    )


def shuffle():
    rows = np.arange(QUARTERS * 2 * SLOTS).reshape(-1, 2, QUARTERS, CAP)
    order = rows.transpose(2, 0, 1, 3).reshape(-1)
    return jnp.asarray(np.eye(order.size)[order], jnp.bfloat16)


def permuted(matrix, rows):
    return jnp.dot(matrix, rows, preferred_element_type=jnp.float32).astype(jnp.bfloat16)


def dispatch(packed):
    here, there = jnp.split(packed, 2)
    there = send(there, SWAP_Y)
    units = [jnp.concatenate(u) for u in zip(jnp.split(here, PAIRS), jnp.split(there, PAIRS))]
    mine = [units[0]] + [send(units[r], ENTER[r]) for r in (1, 2, 3)]
    pair = [send(u, SWAP_PAIR) for u in mine]
    chip = whole_rows(permuted(shuffle(), jnp.concatenate(mine + pair)))
    return jnp.concatenate([chip, send(chip, SWAP_CORE)])


def add(a, b):
    return (a.astype(jnp.float32) + b.astype(jnp.float32)).astype(jnp.bfloat16)


def give_back(parts, lanes=None):
    rows = 2 * SLOTS
    if lanes is not None:
        parts = jnp.concatenate([parts, lanes], axis=1)
    chip = add(parts[:rows], send(parts[rows:], SWAP_CORE))
    if lanes is None:
        chip = quarter_rows(chip)
    else:
        width = parts.shape[1] - lanes.shape[1]
        more = jnp.pad(chip[:, width:], ((0, (QUARTERS - 1) * rows), (0, 0)))
        chip = jnp.concatenate([quarter_rows(chip[:, :width]), more], axis=1)
    mine, pair = jnp.split(permuted(shuffle().T, chip), 2)
    mine = add(mine, send(pair, SWAP_PAIR))
    mine = jnp.split(mine, PAIRS)
    units = [mine[0]] + [send(mine[r], back_of(ENTER[r])) for r in (1, 2, 3)]
    here, there = zip(*[jnp.split(u, 2) for u in units])
    return jnp.concatenate(here + (send(jnp.concatenate(there), SWAP_Y),))


def expert_forward(rows, gate_cols, up_cols, down_rows):
    gate_proj = jnp.dot(rows, gate_cols, preferred_element_type=jnp.float32)
    up_proj = jnp.dot(rows, up_cols, preferred_element_type=jnp.float32)
    hidden = (jax.nn.silu(gate_proj) * up_proj).astype(jnp.bfloat16)
    return jnp.dot(hidden, down_rows, preferred_element_type=jnp.float32).astype(jnp.bfloat16)


def expert_backward(rows, grads, gate_cols, up_cols, down_rows):
    dims = (((1,), (1,)), ((), ()))
    gate_proj = jnp.dot(rows, gate_cols, preferred_element_type=jnp.float32)
    up_proj = jnp.dot(rows, up_cols, preferred_element_type=jnp.float32)
    sigmoid_gate = jax.nn.sigmoid(gate_proj)
    activated = gate_proj * sigmoid_gate
    hidden = (activated * up_proj).astype(jnp.bfloat16)
    grad_hidden = lax.dot_general(grads, down_rows, dims, preferred_element_type=jnp.float32)
    dots = jnp.sum(hidden.astype(jnp.float32) * grad_hidden, axis=-1)
    grad_gate = (
        grad_hidden * up_proj * sigmoid_gate * (1.0 + gate_proj * (1.0 - sigmoid_gate))
    ).astype(jnp.bfloat16)
    grad_up = (grad_hidden * activated).astype(jnp.bfloat16)
    grad_rows = lax.dot_general(grad_gate, gate_cols, dims, preferred_element_type=jnp.float32)
    grad_rows = grad_rows + lax.dot_general(
        grad_up, up_cols, dims, preferred_element_type=jnp.float32
    )
    column = lax.axis_index("ep") % 4
    lanes = jnp.where(jnp.arange(128)[None, :] == column, dots[:, None], 0.0)
    return grad_rows.astype(jnp.bfloat16), lanes.astype(jnp.bfloat16)


def local(
    act_fwd, act_saved, cot_in, routes_fwd, routes_bwd, w_gate, w_up, w_down, router, norm_gain
):
    gate_cols = w_gate[0]
    up_cols = w_up[0]
    down_rows = w_down[0]
    table = router[0]
    gain = norm_gain[0]
    fwd_rows = act_fwd[0]
    saved_rows = act_saved[0]
    grad_in = cot_in[0]
    width = fwd_rows.shape[1]

    slots_bwd = slots_of(routes_bwd[0])
    slots_fwd = slots_of(routes_fwd[0])
    ones = jnp.ones(slots_bwd.shape, jnp.float32)
    placer_bwd = placing(slots_bwd, ones)
    placer_fwd = placing(slots_fwd, ones).astype(jnp.bfloat16)
    packer_bwd = placer_bwd.astype(jnp.bfloat16)
    arrived_grad = dispatch(pack_rows(packer_bwd, grad_in))
    normed_bwd, inverse_bwd = normalize(saved_rows, gain)
    arrived_bwd = dispatch(pack_rows(packer_bwd, normed_bwd))
    normed_fwd, _ = normalize(fwd_rows, gain)
    arrived_fwd = dispatch(pack_rows(placer_fwd, normed_fwd))
    weights_bwd, chosen, summed, onehot = gate_values(normed_bwd, table, routes_bwd[0])
    weights_fwd = gate_values(normed_fwd, table, routes_fwd[0])[0]

    back_bwd = give_back(*expert_backward(arrived_bwd, arrived_grad, gate_cols, up_cols, down_rows))
    back_fwd = give_back(expert_forward(arrived_fwd, gate_cols, up_cols, down_rows))

    def mixed(slots, weights, back):
        return whole_rows(
            lax.dot_general(
                placing(slots, weights),
                back.astype(jnp.float32),
                (((0,), (0,)), ((), ())),
                precision=lax.Precision.HIGHEST,
            )
        )

    quarter = width // QUARTERS
    dot_rows = jnp.sum(back_bwd[:, quarter:].astype(jnp.float32), axis=-1, keepdims=True)
    slot_dots = jnp.sum(dot_rows.reshape(EXPERTS, QUARTERS, CAP), axis=1).reshape(SLOTS)
    slot_range = jnp.arange(SLOTS, dtype=jnp.int32)[None, None, :]
    dot_assign = jnp.sum(jnp.where(slots_bwd[:, :, None] == slot_range, slot_dots, 0.0), axis=-1)
    grad_normed = mixed(slots_bwd, weights_bwd, back_bwd[:, :quarter])
    cross = jnp.sum(dot_assign * chosen, axis=-1, keepdims=True)
    grad_aff = routed_scale * (dot_assign / summed - cross / (summed * summed))
    grad_logit = grad_aff * chosen * (1.0 - chosen)
    grad_table = jnp.sum(onehot * grad_logit[:, :, None], axis=1)
    grad_normed = grad_normed + lax.dot_general(
        grad_table, table, (((1,), (1,)), ((), ())), precision=lax.Precision.HIGHEST
    )
    scaled = gain * grad_normed
    widened = saved_rows.astype(jnp.float32)
    grad_input = (
        inverse_bwd * scaled
        - widened
        * inverse_bwd
        * inverse_bwd
        * inverse_bwd
        * jnp.mean(widened * scaled, axis=-1, keepdims=True)
    )
    result_bwd = (grad_in.astype(jnp.float32) + grad_input).astype(jnp.bfloat16)
    cot_next = from_behind(result_bwd[None], "section", -1)

    expert_out = mixed(slots_fwd, weights_fwd, back_fwd)
    result_fwd = (fwd_rows.astype(jnp.float32) + expert_out).astype(jnp.bfloat16)
    fwd_next = from_behind(result_fwd[None], "section", 1)
    return (fwd_next, cot_next)


def solution(mesh):
    return jax.shard_map(
        local,
        mesh=mesh,
        in_specs=(
            P("section", "ep", None),
            P("section", "ep", None),
            P("section", "ep", None),
            P("section", "ep", None),
            P("section", "ep", None),
            P("section", None, "ep"),
            P("section", None, "ep"),
            P("section", "ep", None),
            P("section", None, None),
            P("section", None),
        ),
        out_specs=(P("section", "ep", None), P("section", "ep", None)),
        check_vma=False,
    )
```

```python
import functools

import jax
import jax.numpy as jnp
from jax import lax
from jax.experimental import pallas as pl
from jax.experimental.pallas import tpu as pltpu
from jax.sharding import PartitionSpec as P

TOPK = 2
CAP = 6
PAIRS = 4
SOURCES = 4
UNIT = SOURCES * CAP
PIECE = 2 * UNIT
LANES = 128

routed_scale = 2.5


def place_of(index):
    return index // 16, index // 2 % 8, index % 2


def route_of(step):
    def target(index):
        y, z, core = place_of(index)
        sign = -1 if z % 2 else 1
        y, z, core = step(y, z, core, sign)
        return y * 16 + z % 8 * 2 + core

    return [(i, target(i)) for i in range(32)]


def back_of(route):
    return [(b, a) for a, b in route]


SWAP_Y = route_of(lambda y, z, core, sign: (1 - y, z, core))
SWAP_CORE = route_of(lambda y, z, core, sign: (y, z, 1 - core))
SWAP_PAIR = route_of(lambda y, z, core, sign: (y, z + sign, core))
NEAR = route_of(lambda y, z, core, sign: (y, z - sign, core))
FAR = route_of(lambda y, z, core, sign: (y, z + 2 * sign, core))


def send(block, route):
    return lax.ppermute(block, "ep", route)


def after(block, *earlier):
    return lax.optimization_barrier((block,) + earlier)[0]


def from_behind(block, axis, distance):
    devices = range(lax.axis_size(axis))
    route = [((i - distance) % len(devices), i) for i in devices]
    return lax.ppermute(block, axis, route)


def normalize(activations, gain):
    widened = activations.astype(jnp.float32)
    inverse = lax.rsqrt(jnp.mean(widened * widened, axis=-1, keepdims=True) + 1e-06)
    return ((widened * inverse * gain).astype(jnp.bfloat16), inverse)


def gate_values(normed, table, expert_ids):
    logits = jnp.dot(normed.astype(jnp.float32), table, precision=lax.Precision.HIGHEST)
    affinity = jax.nn.sigmoid(logits)
    onehot = (
        expert_ids[:, :, None] == jnp.arange(table.shape[1], dtype=jnp.int32)[None, None, :]
    ).astype(jnp.float32)
    chosen = jnp.sum(onehot * affinity[:, None, :], axis=-1)
    summed = jnp.sum(chosen, axis=-1, keepdims=True)
    return (routed_scale * chosen / summed, chosen, summed, onehot)


def in_core_order(mine, other, core):
    return jnp.where(core == 0, jnp.concatenate([mine, other]), jnp.concatenate([other, mine]))


def small_to_all(values, core):
    both = in_core_order(values, send(values, SWAP_CORE), core)
    return jnp.concatenate([both, send(both, SWAP_Y)])


def half_of(rows, which):
    half = rows.shape[1] // 2
    return lax.dynamic_slice_in_dim(rows, which * half, half, axis=1)


def share_tokens(rows, core):
    both = in_core_order(half_of(rows, core), send(half_of(rows, 1 - core), SWAP_CORE), core)
    return jnp.concatenate([both, send(both, SWAP_Y)])


def slots_of(expert_ids, y, z):
    ids = expert_ids.reshape(SOURCES, -1)
    count = jnp.arange(ids.shape[1], dtype=jnp.int32)
    earlier = (ids[:, :, None] == ids[:, None, :]) & (count[None, None, :] < count[None, :, None])
    slot = jnp.sum(earlier.astype(jnp.int32), axis=2)
    away = (ids % PAIRS - z // 2) % PAIRS
    role = jnp.where(z % 2 == 1, (PAIRS - away) % PAIRS, away)
    unit = jnp.where(role == 2, 3, jnp.where(role == 3, 2, role))
    source = jnp.arange(SOURCES, dtype=jnp.int32)[:, None]
    row = unit * UNIT + source * CAP + slot
    return jnp.where(ids // PAIRS == y, row, -1).reshape(expert_ids.shape)


def pack(slots, tokens):
    def piece(first):
        row = first + jnp.arange(PIECE, dtype=jnp.int32)[:, None]
        hit = (row == slots[None, :, 0]) | (row == slots[None, :, 1])
        return jnp.dot(
            hit.astype(jnp.bfloat16), tokens, preferred_element_type=jnp.float32
        ).astype(jnp.bfloat16)

    return piece(0), piece(PIECE)


def dispatch(kept, near, first_after):
    came = send(after(near, *first_after), NEAR)
    mine = jnp.concatenate([kept[:UNIT], came[:UNIT]])
    onward = jnp.concatenate([kept[UNIT:], came[UNIT:]])
    far = send(onward, FAR)
    pieces = [mine, far, send(mine, SWAP_PAIR), send(far, SWAP_PAIR)]
    return pieces, [send(p, SWAP_CORE) for p in pieces], far


def add(a, b):
    return (a.astype(jnp.float32) + b.astype(jnp.float32)).astype(jnp.bfloat16)


def give_back(keep_mine, keep_pair, give_mine, give_pair):
    pair = add(keep_pair, send(give_pair, SWAP_CORE))
    mine = add(keep_mine, send(give_mine, SWAP_CORE))
    mine = add(mine, send(pair, SWAP_PAIR))
    kept, far = mine[:PIECE], mine[PIECE:]
    far = send(far, back_of(FAR))
    near = send(jnp.concatenate([kept[UNIT:], far[UNIT:]]), back_of(NEAR))
    return kept, far, near


def mixed(slots, values, pieces, part=slice(None)):
    total = 0.0
    for piece, first, used in zip(pieces, (0, UNIT, PIECE), (UNIT, UNIT, PIECE)):
        column = jnp.arange(PIECE, dtype=jnp.int32)[None, :]
        row = jnp.where(column < used, column + first, -2)
        weight = 0.0
        for k in range(TOPK):
            weight = weight + jnp.where(slots[:, k : k + 1] == row, values[:, k : k + 1], 0.0)
        total = total + jnp.dot(
            weight, piece[:, part].astype(jnp.float32), precision=lax.Precision.HIGHEST
        )
    return total


def fetch(sources, rows, sems, first, core):
    half = rows.shape[1] // 2
    copies = []
    for i, source in enumerate(sources):
        side = core if i < 4 else 1 - core
        copies.append(
            pltpu.make_async_copy(
                source,
                rows.at[
                    pl.ds(i % 4 * PIECE, PIECE), pl.ds(pl.multiple_of(side * half, LANES), half)
                ],
                sems.at[first + i],
            )
        )
    for c in copies:
        c.start()
    return copies


STEPS = 4


def fetch_steps(source, target, sems, first):
    step = target.shape[0] // STEPS
    copies = [
        pltpu.make_async_copy(
            source.at[pl.ds(i * step, step)], target.at[pl.ds(i * step, step)], sems.at[first + i]
        )
        for i in range(STEPS)
    ]
    for c in copies:
        c.start()
    return copies


NT = (((1,), (1,)), ((), ()))


def projections(rows, gate_w, up_w, gate_copies, up_copies):
    step = gate_w.shape[0] // STEPS
    gate, up = 0.0, 0.0
    for i in range(STEPS):
        part = slice(i * step, (i + 1) * step)
        gate_copies[i].wait()
        gate = gate + jnp.dot(rows[:, part], gate_w[part], preferred_element_type=jnp.float32)
        up_copies[i].wait()
        up = up + jnp.dot(rows[:, part], up_w[part], preferred_element_type=jnp.float32)
    return gate, up


def column_step(half):
    for step in (512, 256, 128):
        if half % step == 0:
            return step
    return half


def forward_kernel(place, *refs):
    pieces, (w_gate, w_up, w_down), outs = refs[:8], refs[8:11], refs[11:15]
    rows, gate_w, up_w, down_w, hidden, sems = refs[15:]
    core = place[0]
    copies = fetch(pieces, rows, sems, 0, core)
    gate_copies = fetch_steps(w_gate, gate_w, sems, 8)
    up_copies = fetch_steps(w_up, up_w, sems, 8 + STEPS)
    down = pltpu.make_async_copy(w_down, down_w, sems.at[8 + 2 * STEPS])
    down.start()
    for c in copies:
        c.wait()
    gate, up = projections(rows, gate_w, up_w, gate_copies, up_copies)
    hidden[...] = (gate * jax.nn.sigmoid(gate) * up).astype(jnp.bfloat16)
    down.wait()
    half = outs[0].shape[1]
    step = column_step(half)
    count = rows.shape[0] // 2
    for side, mine, pair in ((1 - core, outs[2], outs[3]), (core, outs[0], outs[1])):

        @pl.loop(0, half // step)
        def _(i):
            at = pl.multiple_of(i * step, LANES)
            columns = pl.ds(pl.multiple_of(side * half + at, LANES), step)
            out = jnp.dot(
                hidden[...], down_w[:, columns], preferred_element_type=jnp.float32
            ).astype(jnp.bfloat16)
            mine[:, pl.ds(at, step)] = out[:count]
            pair[:, pl.ds(at, step)] = out[count:]


def backward_kernel(place, *refs):
    xs, ys, (w_gate, w_up, w_down), outs = refs[:8], refs[8:16], refs[16:19], refs[19:23]
    rows, grads, gate_w, up_w, down_w, d_gate, d_up, sems = refs[23:]
    core, block = place[0], place[1]
    y_copies = fetch(ys, grads, sems, 0, core)
    down = pltpu.make_async_copy(w_down, down_w, sems.at[16])
    down.start()
    x_copies = fetch(xs, rows, sems, 8, core)
    gate_copies = fetch_steps(w_gate, gate_w, sems, 17)
    up_copies = fetch_steps(w_up, up_w, sems, 17 + STEPS)
    for c in y_copies:
        c.wait()
    down.wait()
    d_hidden = lax.dot_general(grads[...], down_w[...], NT, preferred_element_type=jnp.float32)
    for c in x_copies:
        c.wait()
    gate, up = projections(rows, gate_w, up_w, gate_copies, up_copies)
    sig = jax.nn.sigmoid(gate)
    active = gate * sig
    hidden = (active * up).astype(jnp.bfloat16).astype(jnp.float32)
    dots = jnp.sum(hidden * d_hidden, axis=1, keepdims=True)
    d_gate[...] = (d_hidden * up * sig * (1.0 + gate * (1.0 - sig))).astype(jnp.bfloat16)
    d_up[...] = (d_hidden * active).astype(jnp.bfloat16)
    lane = lax.broadcasted_iota(jnp.int32, (rows.shape[0], LANES), 1)
    lanes = jnp.where(lane == block, dots, 0.0).astype(jnp.bfloat16)
    half = outs[0].shape[1] - LANES
    step = column_step(half)
    count = rows.shape[0] // 2
    for side, mine, pair in ((1 - core, outs[2], outs[3]), (core, outs[0], outs[1])):
        mine[:, half:] = lanes[:count]
        pair[:, half:] = lanes[count:]

        @pl.loop(0, half // step)
        def _(i):
            at = pl.multiple_of(i * step, LANES)
            part = pl.ds(pl.multiple_of(side * half + at, LANES), step)
            out = lax.dot_general(
                d_gate[...], gate_w[part, :], NT, preferred_element_type=jnp.float32
            )
            out = out + lax.dot_general(
                d_up[...], up_w[part, :], NT, preferred_element_type=jnp.float32
            )
            out = out.astype(jnp.bfloat16)
            mine[:, pl.ds(at, step)] = out[:count]
            pair[:, pl.ds(at, step)] = out[count:]


def expert_call(kernel, place, pieces, gate_cols, up_cols, down_rows, sets, extra, scratch):
    width, hidden = gate_cols.shape
    rows = 4 * PIECE
    out = jax.ShapeDtypeStruct((rows // 2, width // 2 + extra), jnp.bfloat16)
    return pl.pallas_call(
        kernel,
        out_shape=(out,) * 4,
        in_specs=[pl.BlockSpec(memory_space=pltpu.SMEM)]
        + [pl.BlockSpec(memory_space=pl.ANY)] * (len(pieces) + 3),
        out_specs=(pl.BlockSpec(memory_space=pltpu.VMEM),) * 4,
        scratch_shapes=[pltpu.VMEM((rows, width), jnp.bfloat16)] * sets
        + [
            pltpu.VMEM((width, hidden), jnp.bfloat16),
            pltpu.VMEM((width, hidden), jnp.bfloat16),
            pltpu.VMEM((hidden, width), jnp.bfloat16),
        ]
        + [pltpu.VMEM((rows, hidden), jnp.bfloat16)] * scratch
        + [pltpu.SemaphoreType.DMA((8 * sets + 1 + 2 * STEPS,))],
        compiler_params=pltpu.CompilerParams(vmem_limit_bytes=40 * 1024 * 1024),
        cost_estimate=pl.CostEstimate(
            flops=2 * rows * width * hidden * 3 * sets,
            bytes_accessed=6 * width * hidden + 4 * rows * width,
            transcendentals=rows * hidden,
        ),
    )(place, *pieces, gate_cols, up_cols, down_rows)


def home_again(mix, extra, core):
    count = mix.shape[0] // SOURCES
    half = mix.shape[1] - extra
    both = mix[: 2 * count] + send(mix[2 * count :].astype(jnp.bfloat16), SWAP_Y).astype(jnp.float32)
    mine = lax.dynamic_slice_in_dim(both, core * count, count)
    other = lax.dynamic_slice_in_dim(both, (1 - core) * count, count)
    got = send(other[:, :half].astype(jnp.bfloat16), SWAP_CORE).astype(jnp.float32)
    kept = mine[:, :half]
    whole = jnp.where(
        core == 0,
        jnp.concatenate([kept, got], axis=1),
        jnp.concatenate([got, kept], axis=1),
    )
    return whole, mine[:, half:]


def local(
    act_fwd, act_saved, cot_in, routes_fwd, routes_bwd, w_gate, w_up, w_down, router, norm_gain
):
    gate_cols = w_gate[0]
    up_cols = w_up[0]
    down_rows = w_down[0]
    table = router[0]
    gain = norm_gain[0]
    fwd_rows = act_fwd[0]
    saved_rows = act_saved[0]
    grad_in = cot_in[0]
    half = fwd_rows.shape[1] // 2
    index = lax.axis_index("ep")
    y, z, core = place_of(index)
    place = jnp.stack([core, index % 4]).astype(jnp.int32)

    ids = small_to_all(jnp.concatenate([routes_bwd[0], routes_fwd[0]], axis=1), core)
    grad_tokens = share_tokens(grad_in, core)
    normed_bwd, inverse_bwd = normalize(saved_rows, gain)
    bwd_tokens = share_tokens(normed_bwd, core)
    normed_fwd, _ = normalize(fwd_rows, gain)
    fwd_tokens = share_tokens(normed_fwd, core)
    slots_bwd = slots_of(ids[:, :TOPK], y, z)
    slots_fwd = slots_of(ids[:, TOPK:], y, z)

    grad_own, grad_other, done = dispatch(*pack(slots_bwd, grad_tokens), ())
    bwd_own, bwd_other, done = dispatch(*pack(slots_bwd, bwd_tokens), (done,))
    fwd_own, fwd_other, done = dispatch(*pack(slots_fwd, fwd_tokens), (done,))

    weights_bwd, chosen, summed, onehot = gate_values(normed_bwd, table, routes_bwd[0])
    weights_fwd = gate_values(normed_fwd, table, routes_fwd[0])[0]
    weights = small_to_all(jnp.concatenate([weights_bwd, weights_fwd], axis=1), core)

    pieces = bwd_own + bwd_other + grad_own + grad_other
    back_bwd = give_back(
        *expert_call(
            backward_kernel, place, pieces, gate_cols, up_cols, down_rows, 2, LANES, 2
        )
    )
    back_fwd = give_back(
        *expert_call(
            forward_kernel, place, fwd_own + fwd_other, gate_cols, up_cols, down_rows, 1, 0, 1
        )
    )

    mix_bwd = mixed(slots_bwd, weights[:, :TOPK], back_bwd, slice(0, half))
    dot_lanes = []
    for k in range(TOPK):
        only = jnp.broadcast_to(jnp.arange(TOPK)[None, :] == k, slots_bwd.shape)
        lanes = mixed(slots_bwd, only.astype(jnp.float32), back_bwd, slice(half, None))
        dot_lanes.append(jnp.sum(lanes, axis=1, keepdims=True))
    dot_lanes = jnp.pad(jnp.concatenate(dot_lanes, axis=1), ((0, 0), (0, LANES - TOPK)))
    grad_normed, dot_assign = home_again(
        jnp.concatenate([mix_bwd, dot_lanes], axis=1), LANES, core
    )
    dot_assign = dot_assign[:, :TOPK]
    cross = jnp.sum(dot_assign * chosen, axis=-1, keepdims=True)
    grad_aff = routed_scale * (dot_assign / summed - cross / (summed * summed))
    grad_logit = grad_aff * chosen * (1.0 - chosen)
    grad_table = jnp.sum(onehot * grad_logit[:, :, None], axis=1)
    grad_normed = grad_normed + lax.dot_general(
        grad_table, table, (((1,), (1,)), ((), ())), precision=lax.Precision.HIGHEST
    )
    scaled = gain * grad_normed
    widened = saved_rows.astype(jnp.float32)
    grad_input = (
        inverse_bwd * scaled
        - widened
        * inverse_bwd
        * inverse_bwd
        * inverse_bwd
        * jnp.mean(widened * scaled, axis=-1, keepdims=True)
    )
    result_bwd = (grad_in.astype(jnp.float32) + grad_input).astype(jnp.bfloat16)
    cot_next = from_behind(result_bwd[None], "section", -1)

    expert_out, _ = home_again(mixed(slots_fwd, weights[:, TOPK:], back_fwd), 0, core)
    result_fwd = (fwd_rows.astype(jnp.float32) + expert_out).astype(jnp.bfloat16)
    fwd_next = from_behind(result_fwd[None], "section", 1)
    return (fwd_next, cot_next)


def solution(mesh):
    return jax.shard_map(
        local,
        mesh=mesh,
        in_specs=(
            P("section", "ep", None),
            P("section", "ep", None),
            P("section", "ep", None),
            P("section", "ep", None),
            P("section", "ep", None),
            P("section", None, "ep"),
            P("section", None, "ep"),
            P("section", "ep", None),
            P("section", None, None),
            P("section", None),
        ),
        out_specs=(P("section", "ep", None), P("section", "ep", None)),
        check_vma=False,
    )
```

```python
import functools

import jax
import jax.numpy as jnp
from jax import lax
from jax.experimental import pallas as pl
from jax.experimental.pallas import tpu as pltpu
from jax.sharding import PartitionSpec as P

TOPK = 2
CAP = 6
PAIRS = 4
SOURCES = 4
UNIT = SOURCES * CAP
PIECE = 2 * UNIT
LANES = 128
VMEM_LIMIT = 16 * 1024 * 1024

routed_scale = 2.5


def place_of(index):
    return index // 16, index // 2 % 8, index % 2


def route_of(step):
    def target(index):
        y, z, core = place_of(index)
        sign = -1 if z % 2 else 1
        y, z, core = step(y, z, core, sign)
        return y * 16 + z % 8 * 2 + core

    return [(i, target(i)) for i in range(32)]


def back_of(route):
    return [(b, a) for a, b in route]


SWAP_Y = route_of(lambda y, z, core, sign: (1 - y, z, core))
SWAP_CORE = route_of(lambda y, z, core, sign: (y, z, 1 - core))
SWAP_PAIR = route_of(lambda y, z, core, sign: (y, z + sign, core))
NEAR = route_of(lambda y, z, core, sign: (y, z - sign, core))
FAR = route_of(lambda y, z, core, sign: (y, z + 2 * sign, core))


def send(block, route):
    return lax.ppermute(block, "ep", route)


def after(block, *earlier):
    return lax.optimization_barrier((block,) + earlier)[0]


def from_behind(block, axis, distance):
    devices = range(lax.axis_size(axis))
    route = [((i - distance) % len(devices), i) for i in devices]
    return lax.ppermute(block, axis, route)


def normalize(activations, gain):
    widened = activations.astype(jnp.float32)
    inverse = lax.rsqrt(jnp.mean(widened * widened, axis=-1, keepdims=True) + 1e-06)
    return ((widened * inverse * gain).astype(jnp.bfloat16), inverse)


def gate_values(normed, table, expert_ids):
    logits = jnp.dot(normed.astype(jnp.float32), table, precision=lax.Precision.HIGHEST)
    affinity = jax.nn.sigmoid(logits)
    onehot = (
        expert_ids[:, :, None] == jnp.arange(table.shape[1], dtype=jnp.int32)[None, None, :]
    ).astype(jnp.float32)
    chosen = jnp.sum(onehot * affinity[:, None, :], axis=-1)
    summed = jnp.sum(chosen, axis=-1, keepdims=True)
    return (routed_scale * chosen / summed, chosen, summed, onehot)


def in_core_order(mine, other, core):
    return jnp.where(core == 0, jnp.concatenate([mine, other]), jnp.concatenate([other, mine]))


def half_of(rows, which):
    half = rows.shape[1] // 2
    return lax.dynamic_slice_in_dim(rows, which * half, half, axis=1)


def share_tokens(rows, core, lanes, *earlier):
    parts = [half_of(rows, core), half_of(rows, 1 - core)]
    if lanes is not None:
        lanes = jnp.pad(lanes.astype(jnp.bfloat16), ((0, 0), (0, LANES - lanes.shape[1])))
        parts = [jnp.concatenate([p, lanes], axis=1) for p in parts]
    got = send(parts[1], SWAP_CORE)
    both = after(in_core_order(parts[0], got, core), *earlier)
    return (both, send(both, SWAP_Y)), got


def three_parts(values):
    first = lax.reduce_precision(values, 8, 7)
    second = lax.reduce_precision(values - first, 8, 7)
    return jnp.concatenate([first, second, values - first - second], axis=1)


def dispatch(kept, near, near_after=(), far_after=()):
    came = send(after(near, *near_after), NEAR)
    mine = jnp.concatenate([kept[:UNIT], came[:UNIT]])
    far = send(after(jnp.concatenate([kept[UNIT:], came[UNIT:]]), *far_after), FAR)
    pieces = [mine, far, send(mine, SWAP_PAIR), send(far, SWAP_PAIR)]
    return pieces + [send(p, SWAP_CORE) for p in pieces], (came, far, pieces[3])


def add(*terms):
    return sum(t.astype(jnp.float32) for t in terms).astype(jnp.bfloat16)


def give_back(give, keep):
    pair = send(add(keep[1], send(give[1], SWAP_CORE)), SWAP_PAIR)
    mine = add(keep[0], send(give[0], SWAP_CORE), pair)
    kept, far = mine[:PIECE], mine[PIECE:]
    far = send(far, back_of(FAR))
    near = send(jnp.concatenate([kept[UNIT:], far[UNIT:]]), back_of(NEAR))
    return kept, far, near


PLACE = pl.BlockSpec(memory_space=pltpu.SMEM)
HERE = pl.BlockSpec(memory_space=pltpu.VMEM)
THERE = pl.BlockSpec(memory_space=pl.ANY)
STEP = 512


def here(array):
    return pltpu.with_memory_space_constraint(array, pltpu.VMEM)


def vmem(shape, dtype):
    return pltpu.VMEM(shape, dtype)


def call(kernel, out_shape, in_specs, scratch_shapes, flops, moved, args):
    args = [here(x) if spec is HERE else x for x, spec in zip(args, in_specs)]
    return pl.pallas_call(
        kernel,
        out_shape=out_shape,
        in_specs=in_specs,
        out_specs=jax.tree.map(lambda _: HERE, out_shape),
        scratch_shapes=scratch_shapes,
        compiler_params=pltpu.CompilerParams(vmem_limit_bytes=VMEM_LIMIT),
        cost_estimate=pl.CostEstimate(flops=flops, bytes_accessed=moved, transcendentals=0),
    )(*args)


def steps_of(size):
    step = STEP if size % STEP == 0 else size
    return [slice(at, at + step) for at in range(0, size, step)]


def slots_of(ids, place):
    y, z = place[2], place[3]
    count = ids[0].shape[0]
    tokens = count // SOURCES
    expert = lax.broadcasted_iota(jnp.int32, (count, LANES), 1)
    onehots = [(i == expert).astype(jnp.float32) for i in ids]
    row = lax.broadcasted_iota(jnp.int32, (count, count), 0)
    column = lax.broadcasted_iota(jnp.int32, (count, count), 1)
    earlier = (column < row) & (column // tokens == row // tokens)
    before = jnp.dot(
        earlier.astype(jnp.float32).astype(jnp.bfloat16),
        sum(onehots).astype(jnp.bfloat16),
        preferred_element_type=jnp.float32,
    )
    source = lax.broadcasted_iota(jnp.int32, (count, 1), 0) // tokens
    slots = []
    for i, onehot in zip(ids, onehots):
        slot = jnp.sum(onehot * before, axis=1, keepdims=True).astype(jnp.int32)
        away = (i + (2 * PAIRS - z // 2)) % PAIRS
        role = jnp.where(z % 2 == 1, (PAIRS - away) % PAIRS, away)
        unit = jnp.where(role == 2, 3, jnp.where(role == 3, 2, role))
        slots.append(jnp.where(i // PAIRS == y, unit * UNIT + source * CAP + slot, -1))
    return slots


def pack_kernel(first, task, place, slots_ref, mine, other, *outs):
    kept, near = outs[:2]
    half = kept.shape[1]
    slots = None
    if task:
        lanes = jnp.concatenate([mine[:, half:], other[:, half:]]).astype(jnp.float32)
    if task == "ids":
        ids = lanes.astype(jnp.int32)
        columns = [ids[:, k : k + 1] for k in range(2 * TOPK)]
        slots = slots_of(columns[:TOPK], place) + slots_of(columns[TOPK:], place)
        for k, slot in enumerate(slots):
            outs[2][:, k : k + 1] = slot
    else:
        slots = [slots_ref[:, k : k + 1] for k in range(2 * TOPK)]
    if task == "values":
        count = 2 * TOPK
        outs[2][...] = lanes[:, :count] + lanes[:, count : 2 * count] + lanes[:, 2 * count : 3 * count]
    tokens = slots[0].shape[0]
    row = lax.broadcasted_iota(jnp.int32, (tokens, LANES), 1)
    hit = (slots[first] == row) | (slots[first + 1] == row)
    placer = hit.astype(jnp.float32).T.astype(jnp.bfloat16)
    for part in steps_of(half):
        rows = jnp.concatenate([mine[:, part], other[:, part]])
        out = jnp.dot(placer, rows, preferred_element_type=jnp.float32).astype(jnp.bfloat16)
        kept[:, part] = out[:PIECE]
        near[:, part] = out[PIECE : 2 * PIECE]


def pack(place, first, tokens, slots=None, task=None):
    mine, other = tokens
    half = mine.shape[1] - (LANES if task else 0)
    count = 2 * mine.shape[0]
    piece = vmem((PIECE, half), jnp.bfloat16)
    outs = (piece, piece)
    if task == "ids":
        outs += (jax.ShapeDtypeStruct((count, 2 * TOPK), jnp.int32),)
        slots = place.reshape(1, -1)
    elif task == "values":
        outs += (jax.ShapeDtypeStruct((count, 2 * TOPK), jnp.float32),)
    return call(
        functools.partial(pack_kernel, first, task),
        outs,
        [PLACE] + [HERE] * 3,
        [],
        2 * LANES * count * half,
        2 * half * (count + 2 * PIECE),
        (place, slots, mine, other),
    )


def load_kernel(axis, source, kept, turned, sems):
    parts = steps_of(source.shape[axis])
    copies = []
    for i, part in enumerate(parts):
        at = (slice(None),) * axis + (pl.ds(part.start, part.stop - part.start),)
        copies.append(pltpu.make_async_copy(source.at[at], kept.at[at], sems.at[i]))
    for c in copies:
        c.start()
    for c, part in zip(copies, parts):
        c.wait()
        if axis == 0:
            turned[:, part] = kept[part].T
        else:
            turned[part] = kept[:, part].T


def load(weight):
    rows, columns = weight.shape
    axis = 0 if rows > columns else 1
    count = len(steps_of(weight.shape[axis]))
    return call(
        functools.partial(load_kernel, axis),
        (vmem((rows, columns), weight.dtype), vmem((columns, rows), weight.dtype)),
        [THERE],
        [pltpu.SemaphoreType.DMA((count,))],
        0,
        6 * rows * columns,
        (pltpu.with_memory_space_constraint(weight, pltpu.HBM),),
    )


def rows_times(pieces, weights, core):
    half = pieces[0].shape[1]
    totals = [0.0] * len(weights)
    for side, four in ((core, pieces[:4]), (1 - core, pieces[4:])):
        rows = jnp.concatenate([p[...] for p in four])
        at = pl.ds(pl.multiple_of(side * half, LANES), half)
        for i, w in enumerate(weights):
            totals[i] = totals[i] + jnp.dot(rows, w[at, :], preferred_element_type=jnp.float32)
    return totals


def hidden_grad_kernel(place, *refs):
    pieces, down_t, out = refs[:8], refs[8], refs[9]
    out[...] = rows_times(pieces, [down_t], place[0])[0]


def hidden_kernel(place, *refs):
    pieces, weights, hidden = refs[:8], refs[8:10], refs[10]
    gate, up = rows_times(pieces, weights, place[0])
    hidden[...] = (gate * jax.nn.sigmoid(gate) * up).astype(jnp.bfloat16)


def gate_grad_kernel(place, d_hidden_ref, *refs):
    pieces, weights, (d_gate, d_up, lanes) = refs[:8], refs[8:10], refs[10:]
    gate, up = rows_times(pieces, weights, place[0])
    d_hidden = d_hidden_ref[...]
    sig = jax.nn.sigmoid(gate)
    active = gate * sig
    hidden = (active * up).astype(jnp.bfloat16).astype(jnp.float32)
    dots = jnp.sum(hidden * d_hidden, axis=1, keepdims=True)
    d_gate[...] = (d_hidden * up * sig * (1.0 + gate * (1.0 - sig))).astype(jnp.bfloat16)
    d_up[...] = (d_hidden * active).astype(jnp.bfloat16)
    lane = lax.broadcasted_iota(jnp.int32, lanes.shape, 1)
    lanes[...] = jnp.where(lane == place[1], dots, 0.0).astype(jnp.bfloat16)


def halves_kernel(count, extra, place, *refs):
    lefts, weights, refs = refs[:count], refs[count : 2 * count], refs[2 * count :]
    outs = refs[1:] if extra else refs
    core = place[0]
    half = weights[0].shape[1] // 2
    rows = lefts[0].shape[0] // 2
    for side, mine, pair in ((1 - core, outs[0], outs[1]), (core, outs[2], outs[3])):
        for part in steps_of(half):
            at = pl.ds(pl.multiple_of(side * half + part.start, LANES), part.stop - part.start)
            out = 0.0
            for left, w in zip(lefts, weights):
                out = out + jnp.dot(left[...], w[:, at], preferred_element_type=jnp.float32)
            out = out.astype(jnp.bfloat16)
            mine[:, part] = out[:rows]
            pair[:, part] = out[rows:]
        if extra:
            mine[:, half:] = refs[0][:rows]
            pair[:, half:] = refs[0][rows:]


def halves(place, lefts, weights, more=()):
    rows, units = lefts[0].shape
    width = weights[0].shape[1]
    extra = sum(m.shape[1] for m in more)
    out = vmem((rows // 2, width // 2 + extra), jnp.bfloat16)
    args = (place, *lefts, *weights, *more)
    outs = call(
        functools.partial(halves_kernel, len(lefts), extra),
        (out,) * 4,
        [PLACE] + [HERE] * (len(args) - 1),
        [],
        2 * rows * width * units * len(lefts),
        2 * width * (rows + units * len(lefts)),
        args,
    )
    return outs[:2], outs[2:]


def expert_forward(place, pieces, gate_w, up_w, down_w):
    width, units = gate_w.shape
    rows = 4 * PIECE
    hidden = call(
        hidden_kernel,
        vmem((rows, units), jnp.bfloat16),
        [PLACE] + [HERE] * 10,
        [],
        4 * rows * width * units,
        2 * width * (rows + 2 * units),
        (place, *pieces, gate_w, up_w),
    )
    return halves(place, [hidden], [down_w])


def expert_backward(place, x_pieces, y_pieces, gate_w, up_w, down_t, gate_t, up_t):
    width, units = gate_w.shape
    rows = 4 * PIECE
    d_hidden = call(
        hidden_grad_kernel,
        vmem((rows, units), jnp.float32),
        [PLACE] + [HERE] * 9,
        [],
        2 * rows * width * units,
        2 * width * (rows + units),
        (place, *y_pieces, down_t),
    )
    narrow = vmem((rows, units), jnp.bfloat16)
    d_gate, d_up, lanes = call(
        gate_grad_kernel,
        (narrow, narrow, vmem((rows, LANES), jnp.bfloat16)),
        [PLACE, HERE] + [HERE] * 10,
        [],
        4 * rows * width * units,
        2 * width * (rows + 2 * units),
        (place, d_hidden, *x_pieces, gate_w, up_w),
    )
    return halves(place, [d_gate, d_up], [gate_t, up_t], (lanes,))


def mix_kernel(first_choice, extra, place, slots, values, kept, far, near, keep, give):
    pieces = ((kept, 0, UNIT), (far, UNIT, UNIT), (near, PIECE, PIECE))
    tokens = slots.shape[0]
    chosen = range(first_choice, first_choice + TOPK)
    half = give.shape[1]
    column = lax.broadcasted_iota(jnp.int32, (tokens, PIECE), 1)
    weights, hits = [], []
    for _, first, used in pieces:
        row = jnp.where(column < used, column + first, -2)
        hit = [slots[:, k : k + 1] == row for k in chosen]
        weight = 0.0
        for k, at in enumerate(chosen):
            weight = weight + jnp.where(hit[k], values[:, at : at + 1], 0.0)
        parts = []
        for _ in range(3):
            parts.append(weight.astype(jnp.bfloat16))
            weight = weight - parts[-1].astype(jnp.float32)
        weights.append(jnp.concatenate(parts))
        hits.append([h.astype(jnp.float32).astype(jnp.bfloat16) for h in hit])
    core = place[0]
    count = tokens // SOURCES

    def split(total):
        first = jnp.concatenate([total[:count], total[2 * count : 3 * count]])
        second = jnp.concatenate([total[count : 2 * count], total[3 * count :]])
        return jnp.where(core == 0, first, second), jnp.where(core == 0, second, first)

    for part in steps_of(half):
        total = 0.0
        for (piece, _, _), weight in zip(pieces, weights):
            total = total + jnp.dot(weight, piece[:, part], preferred_element_type=jnp.float32)
        total = total[:tokens] + total[tokens : 2 * tokens] + total[2 * tokens :]
        mine, other = split(total)
        keep[:, part] = mine
        give[:, part] = other.astype(jnp.bfloat16)
    if extra:
        lane = lax.broadcasted_iota(jnp.int32, (tokens, LANES), 1)
        total = 0.0
        for k in range(TOPK):
            dots = 0.0
            for (piece, _, _), hit in zip(pieces, hits):
                dots = dots + jnp.dot(hit[k], piece[:, half:], preferred_element_type=jnp.float32)
            total = total + jnp.where(lane == k, jnp.sum(dots, axis=1, keepdims=True), 0.0)
        keep[:, half:] = split(total)[0]


def mixed(place, slots, values, first_choice, pieces, extra, core):
    tokens = slots.shape[0]
    half = pieces[0].shape[1] - extra
    keep, give = call(
        functools.partial(mix_kernel, first_choice, extra),
        (
            jax.ShapeDtypeStruct((tokens // 2, half + extra), jnp.float32),
            jax.ShapeDtypeStruct((tokens // 2, half), jnp.bfloat16),
        ),
        [PLACE] + [HERE] * 5,
        [],
        6 * tokens * 3 * PIECE * half,
        2 * 3 * PIECE * half,
        (place, slots, values, *pieces),
    )
    got = send(give, SWAP_CORE).astype(jnp.float32)
    kept = keep[:, :half]
    whole = jnp.where(
        core == 0,
        jnp.concatenate([kept, got], axis=1),
        jnp.concatenate([got, kept], axis=1),
    )
    count = tokens // SOURCES
    if extra:
        whole = jnp.concatenate([whole, keep[:, half:]], axis=1)
    return whole[:count], whole[count:].astype(jnp.bfloat16)


def local(
    act_fwd, act_saved, cot_in, routes_fwd, routes_bwd, w_gate, w_up, w_down, router, norm_gain
):
    gate_cols = w_gate[0]
    up_cols = w_up[0]
    down_rows = w_down[0]
    table = router[0]
    gain = norm_gain[0]
    fwd_rows = act_fwd[0]
    saved_rows = act_saved[0]
    grad_in = cot_in[0]
    index = lax.axis_index("ep")
    y, z, core = place_of(index)
    place = jnp.stack([core, index % 4, y, z]).astype(jnp.int32)

    ids = jnp.concatenate([routes_bwd[0], routes_fwd[0]], axis=1)
    grad_tokens, swapped = share_tokens(grad_in, core, ids)
    grad_kept, grad_near, slots = pack(place, 0, grad_tokens, task="ids")
    grad_pieces, grad_done = dispatch(grad_kept, grad_near)

    normed_bwd, inverse_bwd = normalize(after(saved_rows, swapped), gain)
    bwd_tokens, swapped = share_tokens(normed_bwd, core, None, grad_tokens[1])
    bwd_kept, bwd_near = pack(place, 0, bwd_tokens, slots)
    bwd_pieces, bwd_done = dispatch(bwd_kept, bwd_near, grad_done[:1], grad_done[1:2])

    normed_fwd, _ = normalize(after(fwd_rows, swapped), gain)
    weights_bwd, chosen, summed, onehot = gate_values(normed_bwd, table, routes_bwd[0])
    weights_fwd = gate_values(normed_fwd, table, routes_fwd[0])[0]
    weights = three_parts(jnp.concatenate([weights_bwd, weights_fwd], axis=1))
    fwd_tokens, _ = share_tokens(normed_fwd, core, weights, bwd_tokens[1])
    fwd_kept, fwd_near, values = pack(place, TOPK, fwd_tokens, slots, task="values")
    fwd_pieces, _ = dispatch(fwd_kept, fwd_near, bwd_done[:1], bwd_done[1:2])

    fwd_rows_next = from_behind(after(fwd_rows, grad_done[0]), "section", 1)

    gate_w, gate_t = load(after(gate_cols, grad_done[0]))
    up_w, up_t = load(after(up_cols, grad_done[0]))
    down_w, down_t = load(after(down_rows, grad_done[0]))
    back_bwd = give_back(
        *expert_backward(
            place, bwd_pieces, grad_pieces, gate_w, up_w, down_t, gate_t, up_t
        )
    )
    back_fwd = give_back(*expert_forward(place, fwd_pieces, gate_w, up_w, down_w))

    near, far = mixed(place, slots, values, 0, back_bwd, LANES, core)
    grad_normed = near + send(far, SWAP_Y).astype(jnp.float32)
    dot_assign = grad_normed[:, -LANES:][:, :TOPK]
    grad_normed = grad_normed[:, :-LANES]
    cross = jnp.sum(dot_assign * chosen, axis=-1, keepdims=True)
    grad_aff = routed_scale * (dot_assign / summed - cross / (summed * summed))
    grad_logit = grad_aff * chosen * (1.0 - chosen)
    grad_table = jnp.sum(onehot * grad_logit[:, :, None], axis=1)
    grad_normed = grad_normed + lax.dot_general(
        grad_table, table, (((1,), (1,)), ((), ())), precision=lax.Precision.HIGHEST
    )
    scaled = gain * grad_normed
    widened = saved_rows.astype(jnp.float32)
    grad_input = (
        inverse_bwd * scaled
        - widened
        * inverse_bwd
        * inverse_bwd
        * inverse_bwd
        * jnp.mean(widened * scaled, axis=-1, keepdims=True)
    )
    result_bwd = (grad_in.astype(jnp.float32) + grad_input).astype(jnp.bfloat16)
    cot_next = from_behind(result_bwd[None], "section", -1)

    near, far = mixed(place, slots, values, TOPK, back_fwd, 0, core)
    sections, devices = lax.axis_size("section"), lax.axis_size("ep")
    onward = [
        (s * devices + a, (s + 1) % sections * devices + b) for s in range(sections) for a, b in SWAP_Y
    ]
    near = from_behind(near.astype(jnp.bfloat16), "section", 1)
    far = lax.ppermute(far, ("section", "ep"), onward)
    expert_out = near.astype(jnp.float32) + far.astype(jnp.float32)
    fwd_next = (fwd_rows_next.astype(jnp.float32) + expert_out).astype(jnp.bfloat16)[None]
    return (fwd_next, cot_next)


def solution(mesh):
    return jax.shard_map(
        local,
        mesh=mesh,
        in_specs=(
            P("section", "ep", None),
            P("section", "ep", None),
            P("section", "ep", None),
            P("section", "ep", None),
            P("section", "ep", None),
            P("section", None, "ep"),
            P("section", None, "ep"),
            P("section", "ep", None),
            P("section", None, None),
            P("section", None),
        ),
        out_specs=(P("section", "ep", None), P("section", "ep", None)),
        check_vma=False,
    )
```

```python
import functools

import jax
import jax.numpy as jnp
from jax import lax
from jax.experimental import pallas as pl
from jax.experimental.pallas import tpu as pltpu
from jax.sharding import PartitionSpec as P

TOPK = 2
CAP = 6
PAIRS = 4
SOURCES = 4
UNIT = SOURCES * CAP
PIECE = 2 * UNIT
LANES = 128
VMEM_LIMIT = 16 * 1024 * 1024

routed_scale = 2.5


def place_of(index):
    return index // 16, index // 2 % 8, index % 2


def route_of(step):
    def target(index):
        y, z, core = place_of(index)
        sign = -1 if z % 2 else 1
        y, z, core = step(y, z, core, sign)
        return y * 16 + z % 8 * 2 + core

    return [(i, target(i)) for i in range(32)]


def back_of(route):
    return [(b, a) for a, b in route]


SWAP_Y = route_of(lambda y, z, core, sign: (1 - y, z, core))
SWAP_CORE = route_of(lambda y, z, core, sign: (y, z, 1 - core))
SWAP_PAIR = route_of(lambda y, z, core, sign: (y, z + sign, core))
NEAR = route_of(lambda y, z, core, sign: (y, z - sign, core))
FAR = route_of(lambda y, z, core, sign: (y, z + 2 * sign, core))
NEAR_FAR = route_of(lambda y, z, core, sign: (y, z - 3 * sign, core))


def send(block, route):
    return lax.ppermute(block, "ep", route)


def after(block, *earlier):
    return lax.optimization_barrier((block,) + earlier)[0]


def from_behind(block, axis, distance):
    devices = range(lax.axis_size(axis))
    route = [((i - distance) % len(devices), i) for i in devices]
    return lax.ppermute(block, axis, route)


def normalize(activations, gain):
    widened = activations.astype(jnp.float32)
    inverse = lax.rsqrt(jnp.mean(widened * widened, axis=-1, keepdims=True) + 1e-06)
    return ((widened * inverse * gain).astype(jnp.bfloat16), inverse)


def gate_values(normed, table, expert_ids):
    logits = jnp.dot(normed.astype(jnp.float32), table, precision=lax.Precision.HIGHEST)
    affinity = jax.nn.sigmoid(logits)
    onehot = (
        expert_ids[:, :, None] == jnp.arange(table.shape[1], dtype=jnp.int32)[None, None, :]
    ).astype(jnp.float32)
    chosen = jnp.sum(onehot * affinity[:, None, :], axis=-1)
    summed = jnp.sum(chosen, axis=-1, keepdims=True)
    return (routed_scale * chosen / summed, chosen, summed, onehot)


def in_core_order(mine, other, core):
    return jnp.where(core == 0, jnp.concatenate([mine, other]), jnp.concatenate([other, mine]))


def half_of(rows, which):
    half = rows.shape[1] // 2
    return lax.dynamic_slice_in_dim(rows, which * half, half, axis=1)


def share_cores(rows, core, lanes=None):
    parts = [half_of(rows, core), half_of(rows, 1 - core)]
    if lanes is not None:
        lanes = jnp.pad(lanes.astype(jnp.bfloat16), ((0, 0), (0, LANES - lanes.shape[1])))
        parts = [jnp.concatenate([p, lanes], axis=1) for p in parts]
    return in_core_order(parts[0], send(parts[1], SWAP_CORE), core)


def three_parts(values):
    first = lax.reduce_precision(values, 8, 7)
    second = lax.reduce_precision(values - first, 8, 7)
    return jnp.concatenate([first, second, values - first - second], axis=1)


def enter(kept, near, wait=()):
    came = after(send(near, NEAR), *wait)
    mine = jnp.concatenate([kept[:UNIT], came[:UNIT]])
    return mine, jnp.concatenate([kept[UNIT:], came[UNIT:]])


def spread(mine, onward, far_wait=(), whole=False):
    far = after(send(onward, FAR), *far_wait)
    chip = jnp.concatenate([mine, far])
    if whole:
        return chip, send(chip, SWAP_PAIR), far
    return chip, jnp.concatenate([send(mine, SWAP_PAIR), send(far, SWAP_PAIR)]), far


def both_halves(chip, pair):
    return [chip, pair, send(chip, SWAP_CORE), send(pair, SWAP_CORE)]


def add(*terms):
    return sum(t.astype(jnp.float32) for t in terms).astype(jnp.bfloat16)


def for_pair(give, keep):
    return add(keep[1], send(give[1], SWAP_CORE))


def give_back(mine):
    kept, far = mine[:PIECE], mine[PIECE:]
    far = jnp.concatenate([send(far[:UNIT], back_of(FAR)), send(far[UNIT:], back_of(NEAR_FAR))])
    near = jnp.concatenate([send(kept[UNIT:], back_of(NEAR)), far[UNIT:]])
    return kept, far, near


PLACE = pl.BlockSpec(memory_space=pltpu.SMEM)
HERE = pl.BlockSpec(memory_space=pltpu.VMEM)
THERE = pl.BlockSpec(memory_space=pl.ANY)
STEP = 512


def here(array):
    return pltpu.with_memory_space_constraint(array, pltpu.VMEM)


def vmem(shape, dtype):
    return pltpu.VMEM(shape, dtype)


def call(kernel, out_shape, in_specs, scratch_shapes, flops, moved, args):
    args = [here(x) if spec is HERE else x for x, spec in zip(args, in_specs)]
    return pl.pallas_call(
        kernel,
        out_shape=out_shape,
        in_specs=in_specs,
        out_specs=jax.tree.map(lambda _: HERE, out_shape),
        scratch_shapes=scratch_shapes,
        compiler_params=pltpu.CompilerParams(vmem_limit_bytes=VMEM_LIMIT),
        cost_estimate=pl.CostEstimate(flops=flops, bytes_accessed=moved, transcendentals=0),
    )(*args)


def steps_of(size):
    step = STEP if size % STEP == 0 else size
    return [slice(at, at + step) for at in range(0, size, step)]


def slots_of(ids, place):
    y, z = place[2], place[3]
    count = ids[0].shape[0]
    tokens = count // SOURCES
    expert = lax.broadcasted_iota(jnp.int32, (count, LANES), 1)
    onehots = [(i == expert).astype(jnp.float32) for i in ids]
    row = lax.broadcasted_iota(jnp.int32, (count, count), 0)
    column = lax.broadcasted_iota(jnp.int32, (count, count), 1)
    earlier = (column < row) & (column // tokens == row // tokens)
    before = jnp.dot(
        earlier.astype(jnp.float32).astype(jnp.bfloat16),
        sum(onehots).astype(jnp.bfloat16),
        preferred_element_type=jnp.float32,
    )
    source = lax.broadcasted_iota(jnp.int32, (count, 1), 0) // tokens
    slots = []
    for i, onehot in zip(ids, onehots):
        slot = jnp.sum(onehot * before, axis=1, keepdims=True).astype(jnp.int32)
        away = (i + (2 * PAIRS - z // 2)) % PAIRS
        role = jnp.where(z % 2 == 1, (PAIRS - away) % PAIRS, away)
        unit = jnp.where(role == 2, 3, jnp.where(role == 3, 2, role))
        slots.append(jnp.where(i // PAIRS == y, unit * UNIT + source * CAP + slot, -1))
    return slots


def pack_kernel(first, task, place, slots_ref, mine, other, *outs):
    kept, near = outs[:2]
    half = kept.shape[1]
    slots = None
    if task:
        lanes = jnp.concatenate([mine[:, half:], other[:, half:]]).astype(jnp.float32)
    if task == "ids":
        ids = lanes.astype(jnp.int32)
        columns = [ids[:, k : k + 1] for k in range(2 * TOPK)]
        slots = slots_of(columns[:TOPK], place) + slots_of(columns[TOPK:], place)
        for k, slot in enumerate(slots):
            outs[2][:, k : k + 1] = slot
    else:
        slots = [slots_ref[:, k : k + 1] for k in range(2 * TOPK)]
    if task == "values":
        count = 2 * TOPK
        outs[2][...] = lanes[:, :count] + lanes[:, count : 2 * count] + lanes[:, 2 * count : 3 * count]
    tokens = slots[0].shape[0]
    row = lax.broadcasted_iota(jnp.int32, (tokens, LANES), 1)
    hit = (slots[first] == row) | (slots[first + 1] == row)
    placer = hit.astype(jnp.float32).T.astype(jnp.bfloat16)
    for part in steps_of(half):
        rows = jnp.concatenate([mine[:, part], other[:, part]])
        out = jnp.dot(placer, rows, preferred_element_type=jnp.float32).astype(jnp.bfloat16)
        kept[:, part] = out[:PIECE]
        near[:, part] = out[PIECE : 2 * PIECE]


def pack(place, first, tokens, slots=None, task=None):
    mine, other = tokens
    half = mine.shape[1] - (LANES if task else 0)
    count = 2 * mine.shape[0]
    piece = vmem((PIECE, half), jnp.bfloat16)
    outs = (piece, piece)
    if task == "ids":
        outs += (jax.ShapeDtypeStruct((count, 2 * TOPK), jnp.int32),)
        slots = place.reshape(1, -1)
    elif task == "values":
        outs += (jax.ShapeDtypeStruct((count, 2 * TOPK), jnp.float32),)
    return call(
        functools.partial(pack_kernel, first, task),
        outs,
        [PLACE] + [HERE] * 3,
        [],
        2 * LANES * count * half,
        2 * half * (count + 2 * PIECE),
        (place, slots, mine, other),
    )


def load_kernel(axis, source, kept, turned, sems):
    parts = steps_of(source.shape[axis])
    copies = []
    for i, part in enumerate(parts):
        at = (slice(None),) * axis + (pl.ds(part.start, part.stop - part.start),)
        copies.append(pltpu.make_async_copy(source.at[at], kept.at[at], sems.at[i]))
    for c in copies:
        c.start()
    for c, part in zip(copies, parts):
        c.wait()
        if axis == 0:
            turned[:, part] = kept[part].T
        else:
            turned[part] = kept[:, part].T


def load(weight):
    rows, columns = weight.shape
    axis = 0 if rows > columns else 1
    count = len(steps_of(weight.shape[axis]))
    return call(
        functools.partial(load_kernel, axis),
        (vmem((rows, columns), weight.dtype), vmem((columns, rows), weight.dtype)),
        [THERE],
        [pltpu.SemaphoreType.DMA((count,))],
        0,
        6 * rows * columns,
        (pltpu.with_memory_space_constraint(weight, pltpu.HBM),),
    )


def rows_times(pieces, weights, core):
    half = pieces[0].shape[1]
    totals = [0.0] * len(weights)
    for side, both in ((core, pieces[:2]), (1 - core, pieces[2:])):
        rows = jnp.concatenate([p[...] for p in both])
        at = pl.ds(pl.multiple_of(side * half, LANES), half)
        for i, w in enumerate(weights):
            totals[i] = totals[i] + jnp.dot(rows, w[at, :], preferred_element_type=jnp.float32)
    return totals


def hidden_grad_kernel(place, *refs):
    pieces, down_t, out = refs[:4], refs[4], refs[5]
    out[...] = rows_times(pieces, [down_t], place[0])[0]


def hidden_kernel(place, *refs):
    pieces, weights, hidden = refs[:4], refs[4:6], refs[6]
    gate, up = rows_times(pieces, weights, place[0])
    hidden[...] = (gate * jax.nn.sigmoid(gate) * up).astype(jnp.bfloat16)


def gate_grad_kernel(place, d_hidden_ref, *refs):
    pieces, weights, (d_gate, d_up, lanes) = refs[:4], refs[4:6], refs[6:]
    gate, up = rows_times(pieces, weights, place[0])
    d_hidden = d_hidden_ref[...]
    sig = jax.nn.sigmoid(gate)
    active = gate * sig
    hidden = (active * up).astype(jnp.bfloat16).astype(jnp.float32)
    dots = jnp.sum(hidden * d_hidden, axis=1, keepdims=True)
    d_gate[...] = (d_hidden * up * sig * (1.0 + gate * (1.0 - sig))).astype(jnp.bfloat16)
    d_up[...] = (d_hidden * active).astype(jnp.bfloat16)
    lane = lax.broadcasted_iota(jnp.int32, lanes.shape, 1)
    lanes[...] = jnp.where(lane == place[1], dots, 0.0).astype(jnp.bfloat16)


def halves_kernel(count, extra, place, *refs):
    lefts, weights, refs = refs[:count], refs[count : 2 * count], refs[2 * count :]
    outs = refs[1:] if extra else refs
    core = place[0]
    half = weights[0].shape[1] // 2
    rows = lefts[0].shape[0] // 2
    for side, mine, pair in ((1 - core, outs[0], outs[1]), (core, outs[2], outs[3])):
        for part in steps_of(half):
            at = pl.ds(pl.multiple_of(side * half + part.start, LANES), part.stop - part.start)
            out = 0.0
            for left, w in zip(lefts, weights):
                out = out + jnp.dot(left[...], w[:, at], preferred_element_type=jnp.float32)
            out = out.astype(jnp.bfloat16)
            mine[:, part] = out[:rows]
            pair[:, part] = out[rows:]
        if extra:
            mine[:, half:] = refs[0][:rows]
            pair[:, half:] = refs[0][rows:]


def halves(place, lefts, weights, more=()):
    rows, units = lefts[0].shape
    width = weights[0].shape[1]
    extra = sum(m.shape[1] for m in more)
    out = vmem((rows // 2, width // 2 + extra), jnp.bfloat16)
    args = (place, *lefts, *weights, *more)
    outs = call(
        functools.partial(halves_kernel, len(lefts), extra),
        (out,) * 4,
        [PLACE] + [HERE] * (len(args) - 1),
        [],
        2 * rows * width * units * len(lefts),
        2 * width * (rows + units * len(lefts)),
        args,
    )
    return outs[:2], outs[2:]


def expert_forward(place, pieces, gate_w, up_w, down_w):
    width, units = gate_w.shape
    rows = 4 * PIECE
    hidden = call(
        hidden_kernel,
        vmem((rows, units), jnp.bfloat16),
        [PLACE] + [HERE] * 6,
        [],
        4 * rows * width * units,
        2 * width * (rows + 2 * units),
        (place, *pieces, gate_w, up_w),
    )
    return halves(place, [hidden], [down_w])


def expert_backward(place, x_pieces, y_pieces, gate_w, up_w, down_t, gate_t, up_t):
    width, units = gate_w.shape
    rows = 4 * PIECE
    d_hidden = call(
        hidden_grad_kernel,
        vmem((rows, units), jnp.float32),
        [PLACE] + [HERE] * 5,
        [],
        2 * rows * width * units,
        2 * width * (rows + units),
        (place, *y_pieces, down_t),
    )
    narrow = vmem((rows, units), jnp.bfloat16)
    d_gate, d_up, lanes = call(
        gate_grad_kernel,
        (narrow, narrow, vmem((rows, LANES), jnp.bfloat16)),
        [PLACE] + [HERE] * 7,
        [],
        4 * rows * width * units,
        2 * width * (rows + 2 * units),
        (place, d_hidden, *x_pieces, gate_w, up_w),
    )
    return halves(place, [d_gate, d_up], [gate_t, up_t], (lanes,))


def mix_kernel(first_choice, extra, place, slots, values, kept, far, near, keep, give):
    pieces = ((kept, 0, UNIT), (far, UNIT, UNIT), (near, PIECE, PIECE))
    tokens = slots.shape[0]
    chosen = range(first_choice, first_choice + TOPK)
    half = give.shape[1]
    column = lax.broadcasted_iota(jnp.int32, (tokens, PIECE), 1)
    weights, hits = [], []
    for _, first, used in pieces:
        row = jnp.where(column < used, column + first, -2)
        hit = [slots[:, k : k + 1] == row for k in chosen]
        weight = 0.0
        for k, at in enumerate(chosen):
            weight = weight + jnp.where(hit[k], values[:, at : at + 1], 0.0)
        parts = []
        for _ in range(3):
            parts.append(weight.astype(jnp.bfloat16))
            weight = weight - parts[-1].astype(jnp.float32)
        weights.append(jnp.concatenate(parts))
        hits.append([h.astype(jnp.float32).astype(jnp.bfloat16) for h in hit])
    core = place[0]
    count = tokens // SOURCES

    def split(total):
        first = jnp.concatenate([total[:count], total[2 * count : 3 * count]])
        second = jnp.concatenate([total[count : 2 * count], total[3 * count :]])
        return jnp.where(core == 0, first, second), jnp.where(core == 0, second, first)

    for part in steps_of(half):
        total = 0.0
        for (piece, _, _), weight in zip(pieces, weights):
            total = total + jnp.dot(weight, piece[:, part], preferred_element_type=jnp.float32)
        total = total[:tokens] + total[tokens : 2 * tokens] + total[2 * tokens :]
        mine, other = split(total)
        keep[:, part] = mine
        give[:, part] = other.astype(jnp.bfloat16)
    if extra:
        lane = lax.broadcasted_iota(jnp.int32, (tokens, LANES), 1)
        total = 0.0
        for k in range(TOPK):
            dots = 0.0
            for (piece, _, _), hit in zip(pieces, hits):
                dots = dots + jnp.dot(hit[k], piece[:, half:], preferred_element_type=jnp.float32)
            total = total + jnp.where(lane == k, jnp.sum(dots, axis=1, keepdims=True), 0.0)
        keep[:, half:] = split(total)[0]


def mixed(place, slots, values, first_choice, pieces, extra, core):
    tokens = slots.shape[0]
    half = pieces[0].shape[1] - extra
    keep, give = call(
        functools.partial(mix_kernel, first_choice, extra),
        (
            jax.ShapeDtypeStruct((tokens // 2, half + extra), jnp.float32),
            jax.ShapeDtypeStruct((tokens // 2, half), jnp.bfloat16),
        ),
        [PLACE] + [HERE] * 5,
        [],
        6 * tokens * 3 * PIECE * half,
        2 * 3 * PIECE * half,
        (place, slots, values, *pieces),
    )
    got = send(give, SWAP_CORE).astype(jnp.float32)
    kept = keep[:, :half]
    whole = jnp.where(
        core == 0,
        jnp.concatenate([kept, got], axis=1),
        jnp.concatenate([got, kept], axis=1),
    )
    count = tokens // SOURCES
    if extra:
        whole = jnp.concatenate([whole, keep[:, half:]], axis=1)
    return whole[:count], whole[count:].astype(jnp.bfloat16)


def local(
    act_fwd, act_saved, cot_in, routes_fwd, routes_bwd, w_gate, w_up, w_down, router, norm_gain
):
    gate_cols = w_gate[0]
    up_cols = w_up[0]
    down_rows = w_down[0]
    table = router[0]
    gain = norm_gain[0]
    fwd_rows = act_fwd[0]
    saved_rows = act_saved[0]
    grad_in = cot_in[0]
    index = lax.axis_index("ep")
    y, z, core = place_of(index)
    place = jnp.stack([core, index % 4, y, z]).astype(jnp.int32)

    ids = jnp.concatenate([routes_bwd[0], routes_fwd[0]], axis=1)
    grad_mine = share_cores(grad_in, core, ids)
    grad_other = send(grad_mine, SWAP_Y)
    normed_bwd, inverse_bwd = normalize(saved_rows, gain)
    bwd_mine = share_cores(normed_bwd, core)
    grad_kept, grad_near, slots = pack(
        place, 0, (grad_mine, after(grad_other, bwd_mine)), task="ids"
    )
    bwd_mine = after(bwd_mine, grad_near)
    bwd_other = send(bwd_mine, SWAP_Y)

    grad_entered = enter(grad_kept, grad_near)
    bwd_kept, bwd_near = pack(place, 0, (bwd_mine, after(bwd_other, grad_entered[1])), slots)

    normed_fwd, _ = normalize(after(fwd_rows, bwd_near), gain)
    weights_bwd, chosen, summed, onehot = gate_values(
        after(normed_bwd, bwd_near), table, routes_bwd[0]
    )
    weights_fwd = gate_values(normed_fwd, table, routes_fwd[0])[0]
    weights = three_parts(jnp.concatenate([weights_bwd, weights_fwd], axis=1))
    fwd_mine = share_cores(normed_fwd, core, weights)
    fwd_other = send(fwd_mine, SWAP_Y)

    *grad_chip, grad_far = spread(*grad_entered, (fwd_mine,))
    bwd_entered = enter(bwd_kept, bwd_near, (grad_far,))
    gate_w, gate_t = load(after(gate_cols, bwd_entered[1]))
    up_w, up_t = load(after(up_cols, bwd_entered[1]))
    down_w, down_t = load(after(down_rows, bwd_entered[1]))
    fwd_kept, fwd_near, values = pack(
        place, TOPK, (fwd_mine, after(fwd_other, bwd_entered[1])), slots, task="values"
    )
    fwd_entered = enter(fwd_kept, fwd_near)
    bwd_chip, bwd_pair, _ = spread(*bwd_entered, fwd_entered + (gate_w, up_w, down_w))
    fwd_chip, fwd_pair, _ = spread(*fwd_entered, (), True)
    bwd_pair = after(bwd_pair, fwd_chip)
    fwd_rows_next = from_behind(after(fwd_rows, fwd_near), "section", 1)

    shares = expert_backward(
        place, both_halves(bwd_chip, bwd_pair), both_halves(*grad_chip), gate_w, up_w, down_t, gate_t, up_t
    )
    give, keep = shares
    give = [after(g, fwd_pair, fwd_rows_next) for g in give]
    bwd_pair = send(for_pair(give, keep), SWAP_PAIR)
    bwd_rows = add(keep[0], send(give[0], SWAP_CORE), bwd_pair)
    back_bwd = give_back(bwd_rows)
    pieces = both_halves(fwd_chip, fwd_pair)
    give, keep = expert_forward(place, pieces, gate_w, up_w, down_w)
    fwd_pair = after(send(for_pair(give, keep), SWAP_PAIR), bwd_rows)
    fwd_rows = add(keep[0], send(give[0], SWAP_CORE), fwd_pair)
    back_fwd = give_back(fwd_rows)
    back_bwd = (after(back_bwd[0], fwd_rows),) + back_bwd[1:]

    near, far = mixed(place, slots, values, 0, back_bwd, LANES, core)
    grad_normed = near + send(far, SWAP_Y).astype(jnp.float32)
    back_fwd = (back_fwd[0], after(back_fwd[1], grad_normed), back_fwd[2])
    dot_assign = grad_normed[:, -LANES:][:, :TOPK]
    grad_normed = grad_normed[:, :-LANES]
    cross = jnp.sum(dot_assign * chosen, axis=-1, keepdims=True)
    grad_aff = routed_scale * (dot_assign / summed - cross / (summed * summed))
    grad_logit = grad_aff * chosen * (1.0 - chosen)
    grad_table = jnp.sum(onehot * grad_logit[:, :, None], axis=1)
    grad_normed = grad_normed + lax.dot_general(
        grad_table, table, (((1,), (1,)), ((), ())), precision=lax.Precision.HIGHEST
    )
    scaled = gain * grad_normed
    widened = saved_rows.astype(jnp.float32)
    grad_input = (
        inverse_bwd * scaled
        - widened
        * inverse_bwd
        * inverse_bwd
        * inverse_bwd
        * jnp.mean(widened * scaled, axis=-1, keepdims=True)
    )
    result_bwd = (grad_in.astype(jnp.float32) + grad_input).astype(jnp.bfloat16)

    near, far = mixed(place, slots, values, TOPK, back_fwd, 0, core)
    sections, devices = lax.axis_size("section"), lax.axis_size("ep")
    onward = [
        (s * devices + a, (s + 1) % sections * devices + b) for s in range(sections) for a, b in SWAP_Y
    ]
    cot_next = from_behind(after(result_bwd, far)[None], "section", -1)
    near = from_behind(near.astype(jnp.bfloat16), "section", 1)
    far = lax.ppermute(far, ("section", "ep"), onward)
    expert_out = near.astype(jnp.float32) + far.astype(jnp.float32)
    fwd_next = (fwd_rows_next.astype(jnp.float32) + expert_out).astype(jnp.bfloat16)[None]
    return (fwd_next, cot_next)


def solution(mesh):
    return jax.shard_map(
        local,
        mesh=mesh,
        in_specs=(
            P("section", "ep", None),
            P("section", "ep", None),
            P("section", "ep", None),
            P("section", "ep", None),
            P("section", "ep", None),
            P("section", None, "ep"),
            P("section", None, "ep"),
            P("section", "ep", None),
            P("section", None, None),
            P("section", None),
        ),
        out_specs=(P("section", "ep", None), P("section", "ep", None)),
        check_vma=False,
    )
```

```python
import functools

import jax
import jax.numpy as jnp
from jax import lax
from jax.experimental import pallas as pl
from jax.experimental.pallas import tpu as pltpu
from jax.sharding import PartitionSpec as P

TOPK = 2
CAP = 6
PAIRS = 4
SOURCES = 4
UNIT = SOURCES * CAP
PIECE = 2 * UNIT
LANES = 128
VMEM_LIMIT = 16 * 1024 * 1024

routed_scale = 2.5


def place_of(index):
    return index // 16, index // 2 % 8, index % 2


def route_of(step):
    def target(index):
        y, z, core = place_of(index)
        sign = -1 if z % 2 else 1
        y, z, core = step(y, z, core, sign)
        return y * 16 + z % 8 * 2 + core

    return [(i, target(i)) for i in range(32)]


def back_of(route):
    return [(b, a) for a, b in route]


SWAP_Y = route_of(lambda y, z, core, sign: (1 - y, z, core))
SWAP_CORE = route_of(lambda y, z, core, sign: (y, z, 1 - core))
SWAP_PAIR = route_of(lambda y, z, core, sign: (y, z + sign, core))
NEAR = route_of(lambda y, z, core, sign: (y, z - sign, core))
FAR = route_of(lambda y, z, core, sign: (y, z + 2 * sign, core))
NEAR_FAR = route_of(lambda y, z, core, sign: (y, z - 3 * sign, core))


def send(block, route):
    return lax.ppermute(block, "ep", route)


def after(block, *earlier):
    return lax.optimization_barrier((block,) + earlier)[0]


def from_behind(block, axis, distance):
    devices = range(lax.axis_size(axis))
    route = [((i - distance) % len(devices), i) for i in devices]
    return lax.ppermute(block, axis, route)


def normalize(activations, gain):
    widened = activations.astype(jnp.float32)
    inverse = lax.rsqrt(jnp.mean(widened * widened, axis=-1, keepdims=True) + 1e-06)
    return ((widened * inverse * gain).astype(jnp.bfloat16), inverse)


def gate_values(normed, table, expert_ids):
    logits = jnp.dot(normed.astype(jnp.float32), table, precision=lax.Precision.HIGHEST)
    affinity = jax.nn.sigmoid(logits)
    onehot = (
        expert_ids[:, :, None] == jnp.arange(table.shape[1], dtype=jnp.int32)[None, None, :]
    ).astype(jnp.float32)
    chosen = jnp.sum(onehot * affinity[:, None, :], axis=-1)
    summed = jnp.sum(chosen, axis=-1, keepdims=True)
    return (routed_scale * chosen / summed, chosen, summed, onehot)


def in_core_order(mine, other, core):
    return jnp.where(core == 0, jnp.concatenate([mine, other]), jnp.concatenate([other, mine]))


def half_of(rows, which):
    half = rows.shape[1] // 2
    return lax.dynamic_slice_in_dim(rows, which * half, half, axis=1)


def share_cores(rows, core, lanes=None):
    parts = [half_of(rows, core), half_of(rows, 1 - core)]
    if lanes is not None:
        lanes = jnp.pad(lanes.astype(jnp.bfloat16), ((0, 0), (0, LANES - lanes.shape[1])))
        parts = [jnp.concatenate([p, lanes], axis=1) for p in parts]
    return in_core_order(parts[0], send(parts[1], SWAP_CORE), core)


def three_parts(values):
    first = lax.reduce_precision(values, 8, 7)
    second = lax.reduce_precision(values - first, 8, 7)
    return jnp.concatenate([first, second, values - first - second], axis=1)


def enter(kept, near, wait=()):
    came = after(send(near, NEAR), *wait)
    mine = jnp.concatenate([kept[:UNIT], came[:UNIT]])
    return mine, jnp.concatenate([kept[UNIT:], came[UNIT:]])


def spread(mine, onward, far_wait=(), whole=False):
    far = after(send(onward, FAR), *far_wait)
    chip = jnp.concatenate([mine, far])
    if whole:
        return chip, send(chip, SWAP_PAIR), far
    return chip, jnp.concatenate([send(mine, SWAP_PAIR), send(far, SWAP_PAIR)]), far


def both_halves(chip, pair):
    return [chip, pair, send(chip, SWAP_CORE), send(pair, SWAP_CORE)]


def add(*terms):
    return sum(t.astype(jnp.float32) for t in terms).astype(jnp.bfloat16)


def for_pair(give, keep):
    return add(keep[1], send(give[1], SWAP_CORE))


HOME = [[(i, i) for i in range(32)]] + [back_of(route) for route in (FAR, NEAR, NEAR_FAR)]


def give_back(rows):
    kept, near, far, near_far = jnp.split(rows, PAIRS)
    units = [kept, send(far, HOME[1]), send(near, HOME[2]), send(near_far, HOME[3])]
    return jnp.concatenate(units)


def give_back_onward(rows):
    sections = lax.axis_size("section")
    kept, near, far, near_far = jnp.split(rows, PAIRS)
    units = []
    for unit, route in zip((kept, far, near, near_far), HOME):
        onward = [
            (s * 32 + a, (s + 1) % sections * 32 + b) for s in range(sections) for a, b in route
        ]
        units.append(lax.ppermute(unit, ("section", "ep"), onward))
    return jnp.concatenate(units)


PLACE = pl.BlockSpec(memory_space=pltpu.SMEM)
HERE = pl.BlockSpec(memory_space=pltpu.VMEM)
THERE = pl.BlockSpec(memory_space=pl.ANY)
STEP = 512


def here(array):
    return pltpu.with_memory_space_constraint(array, pltpu.VMEM)


def vmem(shape, dtype):
    return pltpu.VMEM(shape, dtype)


def call(kernel, out_shape, in_specs, scratch_shapes, flops, moved, args):
    args = [here(x) if spec is HERE else x for x, spec in zip(args, in_specs)]
    return pl.pallas_call(
        kernel,
        out_shape=out_shape,
        in_specs=in_specs,
        out_specs=jax.tree.map(lambda _: HERE, out_shape),
        scratch_shapes=scratch_shapes,
        compiler_params=pltpu.CompilerParams(vmem_limit_bytes=VMEM_LIMIT),
        cost_estimate=pl.CostEstimate(flops=flops, bytes_accessed=moved, transcendentals=0),
    )(*args)


def steps_of(size):
    step = STEP if size % STEP == 0 else size
    return [slice(at, at + step) for at in range(0, size, step)]


def slots_of(ids, place):
    y, z = place[2], place[3]
    count = ids[0].shape[0]
    tokens = count // SOURCES
    expert = lax.broadcasted_iota(jnp.int32, (count, LANES), 1)
    onehots = [(i == expert).astype(jnp.float32) for i in ids]
    row = lax.broadcasted_iota(jnp.int32, (count, count), 0)
    column = lax.broadcasted_iota(jnp.int32, (count, count), 1)
    earlier = (column < row) & (column // tokens == row // tokens)
    before = jnp.dot(
        earlier.astype(jnp.float32).astype(jnp.bfloat16),
        sum(onehots).astype(jnp.bfloat16),
        preferred_element_type=jnp.float32,
    )
    source = lax.broadcasted_iota(jnp.int32, (count, 1), 0) // tokens
    slots = []
    for i, onehot in zip(ids, onehots):
        slot = jnp.sum(onehot * before, axis=1, keepdims=True).astype(jnp.int32)
        away = (i + (2 * PAIRS - z // 2)) % PAIRS
        role = jnp.where(z % 2 == 1, (PAIRS - away) % PAIRS, away)
        unit = jnp.where(role == 2, 3, jnp.where(role == 3, 2, role))
        slots.append(jnp.where(i // PAIRS == y, unit * UNIT + source * CAP + slot, -1))
    return slots


def pack_kernel(first, task, place, slots_ref, mine, other, *outs):
    kept, near = outs[:2]
    half = kept.shape[1]
    slots = None
    if task:
        lanes = jnp.concatenate([mine[:, half:], other[:, half:]]).astype(jnp.float32)
    if task == "ids":
        ids = lanes.astype(jnp.int32)
        columns = [ids[:, k : k + 1] for k in range(2 * TOPK)]
        slots = slots_of(columns[:TOPK], place) + slots_of(columns[TOPK:], place)
        for k, slot in enumerate(slots):
            outs[2][:, k : k + 1] = slot
    else:
        slots = [slots_ref[:, k : k + 1] for k in range(2 * TOPK)]
    if task == "values":
        count = 2 * TOPK
        outs[2][...] = lanes[:, :count] + lanes[:, count : 2 * count] + lanes[:, 2 * count : 3 * count]
    tokens = slots[0].shape[0]
    row = lax.broadcasted_iota(jnp.int32, (tokens, LANES), 1)
    hit = (slots[first] == row) | (slots[first + 1] == row)
    placer = hit.astype(jnp.float32).T.astype(jnp.bfloat16)
    for part in steps_of(half):
        rows = jnp.concatenate([mine[:, part], other[:, part]])
        out = jnp.dot(placer, rows, preferred_element_type=jnp.float32).astype(jnp.bfloat16)
        kept[:, part] = out[:PIECE]
        near[:, part] = out[PIECE : 2 * PIECE]


def pack(place, first, tokens, slots=None, task=None):
    mine, other = tokens
    half = mine.shape[1] - (LANES if task else 0)
    count = 2 * mine.shape[0]
    piece = vmem((PIECE, half), jnp.bfloat16)
    outs = (piece, piece)
    if task == "ids":
        outs += (jax.ShapeDtypeStruct((count, 2 * TOPK), jnp.int32),)
        slots = place.reshape(1, -1)
    elif task == "values":
        outs += (jax.ShapeDtypeStruct((count, 2 * TOPK), jnp.float32),)
    return call(
        functools.partial(pack_kernel, first, task),
        outs,
        [PLACE] + [HERE] * 3,
        [],
        2 * LANES * count * half,
        2 * half * (count + 2 * PIECE),
        (place, slots, mine, other),
    )


def turn_kernel(weight, turned):
    for part in steps_of(max(weight.shape)):
        if weight.shape[0] > weight.shape[1]:
            turned[:, part] = weight[part].T
        else:
            turned[part] = weight[:, part].T


def turn(weight):
    return call(
        turn_kernel, vmem(weight.shape[::-1], weight.dtype), [HERE], [], 0, 0, (weight,)
    )


def slots_of(ids, place):
    y, z = place[2], place[3]
    count = ids[0].shape[0]
    tokens = count // SOURCES
    expert = lax.broadcasted_iota(jnp.int32, (count, LANES), 1)
    onehots = [(i == expert).astype(jnp.float32) for i in ids]
    row = lax.broadcasted_iota(jnp.int32, (count, count), 0)
    column = lax.broadcasted_iota(jnp.int32, (count, count), 1)
    earlier = (column < row) & (column // tokens == row // tokens)
    before = jnp.dot(
        earlier.astype(jnp.float32).astype(jnp.bfloat16),
        sum(onehots).astype(jnp.bfloat16),
        preferred_element_type=jnp.float32,
    )
    source = lax.broadcasted_iota(jnp.int32, (count, 1), 0) // tokens
    slots = []
    for i, onehot in zip(ids, onehots):
        slot = jnp.sum(onehot * before, axis=1, keepdims=True).astype(jnp.int32)
        away = (i + (2 * PAIRS - z // 2)) % PAIRS
        role = jnp.where(z % 2 == 1, (PAIRS - away) % PAIRS, away)
        unit = jnp.where(role == 2, 3, jnp.where(role == 3, 2, role))
        slots.append(jnp.where(i // PAIRS == y, unit * UNIT + source * CAP + slot, -1))
    return slots


def pack_kernel(first, task, place, slots_ref, mine, other, *outs):
    kept, near = outs[:2]
    half = kept.shape[1]
    slots = None
    if task:
        lanes = jnp.concatenate([mine[:, half:], other[:, half:]]).astype(jnp.float32)
    if task == "ids":
        ids = lanes.astype(jnp.int32)
        columns = [ids[:, k : k + 1] for k in range(2 * TOPK)]
        slots = slots_of(columns[:TOPK], place) + slots_of(columns[TOPK:], place)
        for k, slot in enumerate(slots):
            outs[2][:, k : k + 1] = slot
    else:
        slots = [slots_ref[:, k : k + 1] for k in range(2 * TOPK)]
    if task == "values":
        count = 2 * TOPK
        outs[2][...] = lanes[:, :count] + lanes[:, count : 2 * count] + lanes[:, 2 * count : 3 * count]
    tokens = slots[0].shape[0]
    row = lax.broadcasted_iota(jnp.int32, (tokens, LANES), 1)
    hit = (slots[first] == row) | (slots[first + 1] == row)
    placer = hit.astype(jnp.float32).T.astype(jnp.bfloat16)
    for part in steps_of(half):
        rows = jnp.concatenate([mine[:, part], other[:, part]])
        out = jnp.dot(placer, rows, preferred_element_type=jnp.float32).astype(jnp.bfloat16)
        kept[:, part] = out[:PIECE]
        near[:, part] = out[PIECE : 2 * PIECE]


def pack(place, first, tokens, slots=None, task=None):
    mine, other = tokens
    half = mine.shape[1] - (LANES if task else 0)
    count = 2 * mine.shape[0]
    piece = vmem((PIECE, half), jnp.bfloat16)
    outs = (piece, piece)
    if task == "ids":
        outs += (jax.ShapeDtypeStruct((count, 2 * TOPK), jnp.int32),)
        slots = place.reshape(1, -1)
    elif task == "values":
        outs += (jax.ShapeDtypeStruct((count, 2 * TOPK), jnp.float32),)
    return call(
        functools.partial(pack_kernel, first, task),
        outs,
        [PLACE] + [HERE] * 3,
        [],
        2 * LANES * count * half,
        2 * half * (count + 2 * PIECE),
        (place, slots, mine, other),
    )


def load_kernel(axis, source, kept, turned, sems):
    parts = steps_of(source.shape[axis])
    copies = []
    for i, part in enumerate(parts):
        at = (slice(None),) * axis + (pl.ds(part.start, part.stop - part.start),)
        copies.append(pltpu.make_async_copy(source.at[at], kept.at[at], sems.at[i]))
    for c in copies:
        c.start()
    for c, part in zip(copies, parts):
        c.wait()
        if axis == 0:
            turned[:, part] = kept[part].T
        else:
            turned[part] = kept[:, part].T


def load(weight):
    rows, columns = weight.shape
    axis = 0 if rows > columns else 1
    count = len(steps_of(weight.shape[axis]))
    return call(
        functools.partial(load_kernel, axis),
        (vmem((rows, columns), weight.dtype), vmem((columns, rows), weight.dtype)),
        [THERE],
        [pltpu.SemaphoreType.DMA((count,))],
        0,
        6 * rows * columns,
        (pltpu.with_memory_space_constraint(weight, pltpu.HBM),),
    )


def rows_times(pieces, weights, core):
    half = pieces[0].shape[1]
    totals = [0.0] * len(weights)
    for side, both in ((core, pieces[:2]), (1 - core, pieces[2:])):
        rows = jnp.concatenate([p[...] for p in both])
        at = pl.ds(pl.multiple_of(side * half, LANES), half)
        for i, w in enumerate(weights):
            totals[i] = totals[i] + jnp.dot(rows, w[at, :], preferred_element_type=jnp.float32)
    return totals


def hidden_grad_kernel(place, *refs):
    pieces, down_t, out = refs[:4], refs[4], refs[5]
    out[...] = rows_times(pieces, [down_t], place[0])[0]


def hidden_kernel(place, *refs):
    pieces, weights, hidden = refs[:4], refs[4:6], refs[6]
    gate, up = rows_times(pieces, weights, place[0])
    hidden[...] = (gate * jax.nn.sigmoid(gate) * up).astype(jnp.bfloat16)


def gate_grad_kernel(place, d_hidden_ref, *refs):
    pieces, weights, (d_gate, d_up, lanes) = refs[:4], refs[4:6], refs[6:]
    gate, up = rows_times(pieces, weights, place[0])
    d_hidden = d_hidden_ref[...]
    sig = jax.nn.sigmoid(gate)
    active = gate * sig
    hidden = (active * up).astype(jnp.bfloat16).astype(jnp.float32)
    dots = jnp.sum(hidden * d_hidden, axis=1, keepdims=True)
    d_gate[...] = (d_hidden * up * sig * (1.0 + gate * (1.0 - sig))).astype(jnp.bfloat16)
    d_up[...] = (d_hidden * active).astype(jnp.bfloat16)
    lane = lax.broadcasted_iota(jnp.int32, lanes.shape, 1)
    lanes[...] = jnp.where(lane == place[1], dots, 0.0).astype(jnp.bfloat16)


def halves_kernel(count, extra, place, *refs):
    lefts, weights, refs = refs[:count], refs[count : 2 * count], refs[2 * count :]
    outs = refs[1:] if extra else refs
    core = place[0]
    half = weights[0].shape[1] // 2
    rows = lefts[0].shape[0] // 2
    for side, mine, pair in ((1 - core, outs[0], outs[1]), (core, outs[2], outs[3])):
        for part in steps_of(half):
            at = pl.ds(pl.multiple_of(side * half + part.start, LANES), part.stop - part.start)
            out = 0.0
            for left, w in zip(lefts, weights):
                out = out + jnp.dot(left[...], w[:, at], preferred_element_type=jnp.float32)
            out = out.astype(jnp.bfloat16)
            mine[:, part] = out[:rows]
            pair[:, part] = out[rows:]
        if extra:
            mine[:, half:] = refs[0][:rows]
            pair[:, half:] = refs[0][rows:]


def halves(place, lefts, weights, more=()):
    rows, units = lefts[0].shape
    width = weights[0].shape[1]
    extra = sum(m.shape[1] for m in more)
    out = vmem((rows // 2, width // 2 + extra), jnp.bfloat16)
    args = (place, *lefts, *weights, *more)
    outs = call(
        functools.partial(halves_kernel, len(lefts), extra),
        (out,) * 4,
        [PLACE] + [HERE] * (len(args) - 1),
        [],
        2 * rows * width * units * len(lefts),
        2 * width * (rows + units * len(lefts)),
        args,
    )
    return outs[:2], outs[2:]


def expert_forward(place, pieces, gate_w, up_w, down_w):
    width, units = gate_w.shape
    rows = 4 * PIECE
    hidden = call(
        hidden_kernel,
        vmem((rows, units), jnp.bfloat16),
        [PLACE] + [HERE] * 6,
        [],
        4 * rows * width * units,
        2 * width * (rows + 2 * units),
        (place, *pieces, gate_w, up_w),
    )
    return halves(place, [hidden], [down_w])


def expert_backward(place, x_pieces, y_pieces, gate_w, up_w, down_t, gate_t, up_t):
    width, units = gate_w.shape
    rows = 4 * PIECE
    d_hidden = call(
        hidden_grad_kernel,
        vmem((rows, units), jnp.float32),
        [PLACE] + [HERE] * 5,
        [],
        2 * rows * width * units,
        2 * width * (rows + units),
        (place, *y_pieces, down_t),
    )
    narrow = vmem((rows, units), jnp.bfloat16)
    d_gate, d_up, lanes = call(
        gate_grad_kernel,
        (narrow, narrow, vmem((rows, LANES), jnp.bfloat16)),
        [PLACE] + [HERE] * 7,
        [],
        4 * rows * width * units,
        2 * width * (rows + 2 * units),
        (place, d_hidden, *x_pieces, gate_w, up_w),
    )
    return halves(place, [d_gate, d_up], [gate_t, up_t], (lanes,))


def mix_kernel(first_choice, extra, place, slots, values, rows, keep, give):
    tokens = slots.shape[0]
    chosen = range(first_choice, first_choice + TOPK)
    half = give.shape[1]
    column = lax.broadcasted_iota(jnp.int32, (tokens, rows.shape[0]), 1)
    hits = [slots[:, k : k + 1] == column for k in chosen]
    weight = 0.0
    for k, hit in zip(chosen, hits):
        weight = weight + jnp.where(hit, values[:, k : k + 1], 0.0)
    parts = []
    for _ in range(3):
        parts.append(weight.astype(jnp.bfloat16))
        weight = weight - parts[-1].astype(jnp.float32)
    weight = jnp.concatenate(parts)
    core = place[0]
    count = tokens // SOURCES

    def split(total):
        first = jnp.concatenate([total[:count], total[2 * count : 3 * count]])
        second = jnp.concatenate([total[count : 2 * count], total[3 * count :]])
        return jnp.where(core == 0, first, second), jnp.where(core == 0, second, first)

    for part in steps_of(half):
        total = jnp.dot(weight, rows[:, part], preferred_element_type=jnp.float32)
        total = total[:tokens] + total[tokens : 2 * tokens] + total[2 * tokens :]
        mine, other = split(total)
        keep[:, part] = mine
        give[:, part] = other.astype(jnp.bfloat16)
    if extra:
        lane = lax.broadcasted_iota(jnp.int32, (tokens, LANES), 1)
        total = 0.0
        for k, hit in enumerate(hits):
            dots = jnp.dot(
                hit.astype(jnp.float32).astype(jnp.bfloat16),
                rows[:, half:],
                preferred_element_type=jnp.float32,
            )
            total = total + jnp.where(lane == k, jnp.sum(dots, axis=1, keepdims=True), 0.0)
        keep[:, half:] = split(total)[0]


def mixed(place, slots, values, first_choice, rows, extra, core):
    tokens = slots.shape[0]
    half = rows.shape[1] - extra
    keep, give = call(
        functools.partial(mix_kernel, first_choice, extra),
        (
            jax.ShapeDtypeStruct((tokens // 2, half + extra), jnp.float32),
            jax.ShapeDtypeStruct((tokens // 2, half), jnp.bfloat16),
        ),
        [PLACE] + [HERE] * 3,
        [],
        6 * tokens * 2 * PIECE * half,
        2 * 2 * PIECE * half,
        (place, slots, values, rows),
    )
    got = send(give, SWAP_CORE).astype(jnp.float32)
    kept = keep[:, :half]
    whole = jnp.where(
        core == 0,
        jnp.concatenate([kept, got], axis=1),
        jnp.concatenate([got, kept], axis=1),
    )
    count = tokens // SOURCES
    if extra:
        whole = jnp.concatenate([whole, keep[:, half:]], axis=1)
    return whole[:count], whole[count:].astype(jnp.bfloat16)


def local(
    act_fwd, act_saved, cot_in, routes_fwd, routes_bwd, w_gate, w_up, w_down, router, norm_gain
):
    gate_cols = w_gate[0]
    up_cols = w_up[0]
    down_rows = w_down[0]
    table = router[0]
    gain = norm_gain[0]
    fwd_rows = act_fwd[0]
    saved_rows = act_saved[0]
    grad_in = cot_in[0]
    index = lax.axis_index("ep")
    y, z, core = place_of(index)
    place = jnp.stack([core, index % 4, y, z]).astype(jnp.int32)

    ids = jnp.concatenate([routes_bwd[0], routes_fwd[0]], axis=1)
    grad_mine = share_cores(grad_in, core, ids)
    grad_other = send(grad_mine, SWAP_Y)
    normed_bwd, inverse_bwd = normalize(saved_rows, gain)
    bwd_mine = share_cores(normed_bwd, core)
    grad_kept, grad_near, slots = pack(
        place, 0, (grad_mine, after(grad_other, bwd_mine)), task="ids"
    )
    bwd_mine = after(bwd_mine, grad_near)
    bwd_other = send(bwd_mine, SWAP_Y)

    grad_entered = enter(grad_kept, grad_near)
    bwd_kept, bwd_near = pack(place, 0, (bwd_mine, after(bwd_other, grad_entered[1])), slots)

    normed_fwd, _ = normalize(after(fwd_rows, bwd_near), gain)
    weights_bwd, chosen, summed, onehot = gate_values(
        after(normed_bwd, bwd_near), table, routes_bwd[0]
    )
    weights_fwd = gate_values(normed_fwd, table, routes_fwd[0])[0]
    weights = three_parts(jnp.concatenate([weights_bwd, weights_fwd], axis=1))
    fwd_mine = share_cores(normed_fwd, core, weights)
    fwd_other = send(fwd_mine, SWAP_Y)

    *grad_chip, grad_far = spread(*grad_entered, (fwd_mine,))
    bwd_entered = enter(bwd_kept, bwd_near, (grad_far,))
    gate_t = turn(after(gate_cols, bwd_entered[1]))
    up_t = turn(after(up_cols, bwd_entered[1]))
    down_t = turn(after(down_rows, bwd_entered[1]))
    fwd_kept, fwd_near, values = pack(
        place, TOPK, (fwd_mine, after(fwd_other, bwd_entered[1])), slots, task="values"
    )
    fwd_entered = enter(fwd_kept, fwd_near)
    bwd_chip, bwd_pair, _ = spread(*bwd_entered, fwd_entered + (gate_t, up_t, down_t))
    fwd_chip, fwd_pair, _ = spread(*fwd_entered, (), True)
    bwd_pair = after(bwd_pair, fwd_chip)
    fwd_rows_next = from_behind(after(fwd_rows, fwd_near), "section", 1)
    tables_next = jnp.concatenate([slots.astype(jnp.float32), values], axis=1)
    tables_next = from_behind(tables_next, "section", 1)

    shares = expert_backward(
        place, both_halves(bwd_chip, bwd_pair), both_halves(*grad_chip), gate_cols, up_cols, down_t, gate_t, up_t
    )
    give, keep = shares
    fwd_pair = after(fwd_pair, give[0])
    give = [after(g, fwd_pair) for g in give]
    bwd_pair = send(for_pair(give, keep), SWAP_PAIR)
    bwd_rows = add(keep[0], send(give[0], SWAP_CORE), bwd_pair)
    back_bwd = give_back(bwd_rows)
    pieces = both_halves(fwd_chip, fwd_pair)
    give, keep = expert_forward(place, pieces, gate_cols, up_cols, down_rows)
    give = [after(g, bwd_rows, fwd_rows_next, tables_next) for g in give]
    fwd_pair = send(for_pair(give, keep), SWAP_PAIR)
    fwd_rows = add(keep[0], send(give[0], SWAP_CORE), fwd_pair)
    back_fwd = give_back_onward(fwd_rows)
    back_bwd = after(back_bwd, fwd_rows)

    near, far = mixed(place, slots, values, 0, back_bwd, LANES, core)
    grad_normed = near + send(far, SWAP_Y).astype(jnp.float32)
    dot_assign = grad_normed[:, -LANES:][:, :TOPK]
    grad_normed = grad_normed[:, :-LANES]
    cross = jnp.sum(dot_assign * chosen, axis=-1, keepdims=True)
    grad_aff = routed_scale * (dot_assign / summed - cross / (summed * summed))
    grad_logit = grad_aff * chosen * (1.0 - chosen)
    grad_table = jnp.sum(onehot * grad_logit[:, :, None], axis=1)
    grad_normed = grad_normed + lax.dot_general(
        grad_table, table, (((1,), (1,)), ((), ())), precision=lax.Precision.HIGHEST
    )
    scaled = gain * grad_normed
    widened = saved_rows.astype(jnp.float32)
    grad_input = (
        inverse_bwd * scaled
        - widened
        * inverse_bwd
        * inverse_bwd
        * inverse_bwd
        * jnp.mean(widened * scaled, axis=-1, keepdims=True)
    )
    result_bwd = (grad_in.astype(jnp.float32) + grad_input).astype(jnp.bfloat16)

    cot_next = from_behind(result_bwd[None], "section", -1)

    slots_next = tables_next[:, : 2 * TOPK].astype(jnp.int32)
    values_next = tables_next[:, 2 * TOPK :]
    near, far = mixed(place, slots_next, values_next, TOPK, back_fwd, 0, core)
    expert_out = near + send(far, SWAP_Y).astype(jnp.float32)
    fwd_next = (fwd_rows_next.astype(jnp.float32) + expert_out).astype(jnp.bfloat16)[None]
    return (fwd_next, cot_next)


def solution(mesh):
    return jax.shard_map(
        local,
        mesh=mesh,
        in_specs=(
            P("section", "ep", None),
            P("section", "ep", None),
            P("section", "ep", None),
            P("section", "ep", None),
            P("section", "ep", None),
            P("section", None, "ep"),
            P("section", None, "ep"),
            P("section", "ep", None),
            P("section", None, None),
            P("section", None),
        ),
        out_specs=(P("section", "ep", None), P("section", "ep", None)),
        check_vma=False,
    )
```

```python
import functools

import jax
import jax.numpy as jnp
from jax import lax
from jax.experimental import pallas as pl
from jax.experimental.pallas import tpu as pltpu
from jax.sharding import PartitionSpec as P

TOPK = 2
CAP = 6
PAIRS = 4
SOURCES = 4
UNIT = SOURCES * CAP
PIECE = 2 * UNIT
LANES = 128
VMEM_LIMIT = 16 * 1024 * 1024

routed_scale = 2.5


def place_of(index):
    return index // 16, index // 2 % 8, index % 2


def route_of(step):
    def target(index):
        y, z, core = place_of(index)
        sign = -1 if z % 2 else 1
        y, z, core = step(y, z, core, sign)
        return y * 16 + z % 8 * 2 + core

    return [(i, target(i)) for i in range(32)]


def back_of(route):
    return [(b, a) for a, b in route]


SWAP_Y = route_of(lambda y, z, core, sign: (1 - y, z, core))
SWAP_CORE = route_of(lambda y, z, core, sign: (y, z, 1 - core))
SWAP_PAIR = route_of(lambda y, z, core, sign: (y, z + sign, core))
NEAR = route_of(lambda y, z, core, sign: (y, z - sign, core))
FAR = route_of(lambda y, z, core, sign: (y, z + 2 * sign, core))
NEAR_FAR = route_of(lambda y, z, core, sign: (y, z - 3 * sign, core))


def send(block, route):
    return lax.ppermute(block, "ep", route)


def after(block, *earlier):
    return lax.optimization_barrier((block,) + earlier)[0]


def from_behind(block, axis, distance):
    devices = range(lax.axis_size(axis))
    route = [((i - distance) % len(devices), i) for i in devices]
    return lax.ppermute(block, axis, route)


def normalize(activations, gain):
    widened = activations.astype(jnp.float32)
    inverse = lax.rsqrt(jnp.mean(widened * widened, axis=-1, keepdims=True) + 1e-06)
    return ((widened * inverse * gain).astype(jnp.bfloat16), inverse)


def gate_values(normed, table, expert_ids):
    logits = jnp.dot(normed.astype(jnp.float32), table, precision=lax.Precision.HIGHEST)
    affinity = jax.nn.sigmoid(logits)
    onehot = (
        expert_ids[:, :, None] == jnp.arange(table.shape[1], dtype=jnp.int32)[None, None, :]
    ).astype(jnp.float32)
    chosen = jnp.sum(onehot * affinity[:, None, :], axis=-1)
    summed = jnp.sum(chosen, axis=-1, keepdims=True)
    return (routed_scale * chosen / summed, chosen, summed, onehot)


def in_core_order(mine, other, core):
    return jnp.where(core == 0, jnp.concatenate([mine, other]), jnp.concatenate([other, mine]))


def half_of(rows, which):
    half = rows.shape[1] // 2
    return lax.dynamic_slice_in_dim(rows, which * half, half, axis=1)


def share_cores(rows, core, lanes=None):
    parts = [half_of(rows, core), half_of(rows, 1 - core)]
    if lanes is not None:
        lanes = jnp.pad(lanes.astype(jnp.bfloat16), ((0, 0), (0, LANES - lanes.shape[1])))
        parts = [jnp.concatenate([p, lanes], axis=1) for p in parts]
    return in_core_order(parts[0], send(parts[1], SWAP_CORE), core)


def three_parts(values):
    first = lax.reduce_precision(values, 8, 7)
    second = lax.reduce_precision(values - first, 8, 7)
    return jnp.concatenate([first, second, values - first - second], axis=1)


def enter(kept, near, wait=()):
    came = after(send(near, NEAR), *wait)
    mine = jnp.concatenate([kept[:UNIT], came[:UNIT]])
    return mine, jnp.concatenate([kept[UNIT:], came[UNIT:]])


def spread(mine, onward, far_wait=(), whole=False):
    far = after(send(onward, FAR), *far_wait)
    chip = jnp.concatenate([mine, far])
    if whole:
        return chip, send(chip, SWAP_PAIR), far
    return chip, jnp.concatenate([send(mine, SWAP_PAIR), send(far, SWAP_PAIR)]), far


def both_halves(chip, pair):
    return [chip, pair, send(chip, SWAP_CORE), send(pair, SWAP_CORE)]


def add(*terms):
    return sum(t.astype(jnp.float32) for t in terms).astype(jnp.bfloat16)


def for_pair(give, keep):
    return add(keep[1], send(give[1], SWAP_CORE))


HOME = [[(i, i) for i in range(32)]] + [back_of(route) for route in (FAR, NEAR, NEAR_FAR)]


def give_back(rows):
    kept, near, far, near_far = jnp.split(rows, PAIRS)
    units = [kept, send(far, HOME[1]), send(near, HOME[2]), send(near_far, HOME[3])]
    return jnp.concatenate(units)


def give_back_onward(rows):
    sections = lax.axis_size("section")
    kept, near, far, near_far = jnp.split(rows, PAIRS)
    units = []
    for unit, route in zip((kept, far, near, near_far), HOME):
        onward = [
            (s * 32 + a, (s + 1) % sections * 32 + b) for s in range(sections) for a, b in route
        ]
        units.append(lax.ppermute(unit, ("section", "ep"), onward))
    return jnp.concatenate(units)


PLACE = pl.BlockSpec(memory_space=pltpu.SMEM)
HERE = pl.BlockSpec(memory_space=pltpu.VMEM)
THERE = pl.BlockSpec(memory_space=pl.ANY)
STEP = 512


def here(array):
    return pltpu.with_memory_space_constraint(array, pltpu.VMEM)


def vmem(shape, dtype):
    return pltpu.VMEM(shape, dtype)


def call(kernel, out_shape, in_specs, scratch_shapes, flops, moved, args):
    args = [here(x) if spec is HERE else x for x, spec in zip(args, in_specs)]
    return pl.pallas_call(
        kernel,
        out_shape=out_shape,
        in_specs=in_specs,
        out_specs=jax.tree.map(lambda _: HERE, out_shape),
        scratch_shapes=scratch_shapes,
        compiler_params=pltpu.CompilerParams(vmem_limit_bytes=VMEM_LIMIT),
        cost_estimate=pl.CostEstimate(flops=flops, bytes_accessed=moved, transcendentals=0),
    )(*args)


def steps_of(size):
    step = STEP if size % STEP == 0 else size
    return [slice(at, at + step) for at in range(0, size, step)]


def slots_of(ids, place):
    y, z = place[2], place[3]
    count = ids[0].shape[0]
    tokens = count // SOURCES
    expert = lax.broadcasted_iota(jnp.int32, (count, LANES), 1)
    onehots = [(i == expert).astype(jnp.float32) for i in ids]
    row = lax.broadcasted_iota(jnp.int32, (count, count), 0)
    column = lax.broadcasted_iota(jnp.int32, (count, count), 1)
    earlier = (column < row) & (column // tokens == row // tokens)
    before = jnp.dot(
        earlier.astype(jnp.float32).astype(jnp.bfloat16),
        sum(onehots).astype(jnp.bfloat16),
        preferred_element_type=jnp.float32,
    )
    source = lax.broadcasted_iota(jnp.int32, (count, 1), 0) // tokens
    slots = []
    for i, onehot in zip(ids, onehots):
        slot = jnp.sum(onehot * before, axis=1, keepdims=True).astype(jnp.int32)
        away = (i + (2 * PAIRS - z // 2)) % PAIRS
        role = jnp.where(z % 2 == 1, (PAIRS - away) % PAIRS, away)
        unit = jnp.where(role == 2, 3, jnp.where(role == 3, 2, role))
        slots.append(jnp.where(i // PAIRS == y, unit * UNIT + source * CAP + slot, -1))
    return slots


def pack_kernel(first, task, place, slots_ref, mine, other, *outs):
    kept, near = outs[:2]
    half = kept.shape[1]
    slots = None
    if task:
        lanes = jnp.concatenate([mine[:, half:], other[:, half:]]).astype(jnp.float32)
    if task == "ids":
        ids = lanes.astype(jnp.int32)
        columns = [ids[:, k : k + 1] for k in range(2 * TOPK)]
        slots = slots_of(columns[:TOPK], place) + slots_of(columns[TOPK:], place)
        for k, slot in enumerate(slots):
            outs[2][:, k : k + 1] = slot
    else:
        slots = [slots_ref[:, k : k + 1] for k in range(2 * TOPK)]
    if task == "values":
        count = 2 * TOPK
        outs[2][...] = lanes[:, :count] + lanes[:, count : 2 * count] + lanes[:, 2 * count : 3 * count]
    tokens = slots[0].shape[0]
    row = lax.broadcasted_iota(jnp.int32, (tokens, LANES), 1)
    hit = (slots[first] == row) | (slots[first + 1] == row)
    placer = hit.astype(jnp.float32).T.astype(jnp.bfloat16)
    for part in steps_of(half):
        rows = jnp.concatenate([mine[:, part], other[:, part]])
        out = jnp.dot(placer, rows, preferred_element_type=jnp.float32).astype(jnp.bfloat16)
        kept[:, part] = out[:PIECE]
        near[:, part] = out[PIECE : 2 * PIECE]


def pack(place, first, tokens, slots=None, task=None):
    mine, other = tokens
    half = mine.shape[1] - (LANES if task else 0)
    count = 2 * mine.shape[0]
    piece = vmem((PIECE, half), jnp.bfloat16)
    outs = (piece, piece)
    if task == "ids":
        outs += (jax.ShapeDtypeStruct((count, 2 * TOPK), jnp.int32),)
        slots = place.reshape(1, -1)
    elif task == "values":
        outs += (jax.ShapeDtypeStruct((count, 2 * TOPK), jnp.float32),)
    return call(
        functools.partial(pack_kernel, first, task),
        outs,
        [PLACE] + [HERE] * 3,
        [],
        2 * LANES * count * half,
        2 * half * (count + 2 * PIECE),
        (place, slots, mine, other),
    )


def turn_kernel(weight, turned):
    for part in steps_of(max(weight.shape)):
        if weight.shape[0] > weight.shape[1]:
            turned[:, part] = weight[part].T
        else:
            turned[part] = weight[:, part].T


def turn(weight):
    return call(
        turn_kernel, vmem(weight.shape[::-1], weight.dtype), [HERE], [], 0, 0, (weight,)
    )


def slots_of(ids, place):
    y, z = place[2], place[3]
    count = ids[0].shape[0]
    tokens = count // SOURCES
    expert = lax.broadcasted_iota(jnp.int32, (count, LANES), 1)
    onehots = [(i == expert).astype(jnp.float32) for i in ids]
    row = lax.broadcasted_iota(jnp.int32, (count, count), 0)
    column = lax.broadcasted_iota(jnp.int32, (count, count), 1)
    earlier = (column < row) & (column // tokens == row // tokens)
    before = jnp.dot(
        earlier.astype(jnp.float32).astype(jnp.bfloat16),
        sum(onehots).astype(jnp.bfloat16),
        preferred_element_type=jnp.float32,
    )
    source = lax.broadcasted_iota(jnp.int32, (count, 1), 0) // tokens
    slots = []
    for i, onehot in zip(ids, onehots):
        slot = jnp.sum(onehot * before, axis=1, keepdims=True).astype(jnp.int32)
        away = (i + (2 * PAIRS - z // 2)) % PAIRS
        role = jnp.where(z % 2 == 1, (PAIRS - away) % PAIRS, away)
        unit = jnp.where(role == 2, 3, jnp.where(role == 3, 2, role))
        slots.append(jnp.where(i // PAIRS == y, unit * UNIT + source * CAP + slot, -1))
    return slots


def pack_kernel(first, task, place, slots_ref, mine, other, *outs):
    kept, near = outs[:2]
    half = kept.shape[1]
    slots = None
    if task:
        lanes = jnp.concatenate([mine[:, half:], other[:, half:]]).astype(jnp.float32)
    if task == "ids":
        ids = lanes.astype(jnp.int32)
        columns = [ids[:, k : k + 1] for k in range(2 * TOPK)]
        slots = slots_of(columns[:TOPK], place) + slots_of(columns[TOPK:], place)
        for k, slot in enumerate(slots):
            outs[2][:, k : k + 1] = slot
    else:
        slots = [slots_ref[:, k : k + 1] for k in range(2 * TOPK)]
    if task == "values":
        count = 2 * TOPK
        outs[2][...] = lanes[:, :count] + lanes[:, count : 2 * count] + lanes[:, 2 * count : 3 * count]
    tokens = slots[0].shape[0]
    row = lax.broadcasted_iota(jnp.int32, (tokens, LANES), 1)
    hit = (slots[first] == row) | (slots[first + 1] == row)
    placer = hit.astype(jnp.float32).T.astype(jnp.bfloat16)
    for part in steps_of(half):
        rows = jnp.concatenate([mine[:, part], other[:, part]])
        out = jnp.dot(placer, rows, preferred_element_type=jnp.float32).astype(jnp.bfloat16)
        kept[:, part] = out[:PIECE]
        near[:, part] = out[PIECE : 2 * PIECE]


def pack(place, first, tokens, slots=None, task=None):
    mine, other = tokens
    half = mine.shape[1] - (LANES if task else 0)
    count = 2 * mine.shape[0]
    piece = vmem((PIECE, half), jnp.bfloat16)
    outs = (piece, piece)
    if task == "ids":
        outs += (jax.ShapeDtypeStruct((count, 2 * TOPK), jnp.int32),)
        slots = place.reshape(1, -1)
    elif task == "values":
        outs += (jax.ShapeDtypeStruct((count, 2 * TOPK), jnp.float32),)
    return call(
        functools.partial(pack_kernel, first, task),
        outs,
        [PLACE] + [HERE] * 3,
        [],
        2 * LANES * count * half,
        2 * half * (count + 2 * PIECE),
        (place, slots, mine, other),
    )


def load_kernel(axis, source, kept, turned, sems):
    parts = steps_of(source.shape[axis])
    copies = []
    for i, part in enumerate(parts):
        at = (slice(None),) * axis + (pl.ds(part.start, part.stop - part.start),)
        copies.append(pltpu.make_async_copy(source.at[at], kept.at[at], sems.at[i]))
    for c in copies:
        c.start()
    for c, part in zip(copies, parts):
        c.wait()
        if axis == 0:
            turned[:, part] = kept[part].T
        else:
            turned[part] = kept[:, part].T


def load(weight):
    rows, columns = weight.shape
    axis = 0 if rows > columns else 1
    count = len(steps_of(weight.shape[axis]))
    return call(
        functools.partial(load_kernel, axis),
        (vmem((rows, columns), weight.dtype), vmem((columns, rows), weight.dtype)),
        [THERE],
        [pltpu.SemaphoreType.DMA((count,))],
        0,
        6 * rows * columns,
        (pltpu.with_memory_space_constraint(weight, pltpu.HBM),),
    )


def rows_times(pieces, weights, core):
    half = pieces[0].shape[1]
    totals = [0.0] * len(weights)
    for side, both in ((core, pieces[:2]), (1 - core, pieces[2:])):
        rows = jnp.concatenate([p[...] for p in both])
        at = pl.ds(pl.multiple_of(side * half, LANES), half)
        for i, w in enumerate(weights):
            totals[i] = totals[i] + jnp.dot(rows, w[at, :], preferred_element_type=jnp.float32)
    return totals


def hidden_grad_kernel(place, *refs):
    pieces, down_t, out = refs[:4], refs[4], refs[5]
    out[...] = rows_times(pieces, [down_t], place[0])[0]


def hidden_kernel(place, *refs):
    pieces, weights, hidden = refs[:4], refs[4:6], refs[6]
    gate, up = rows_times(pieces, weights, place[0])
    hidden[...] = (gate * jax.nn.sigmoid(gate) * up).astype(jnp.bfloat16)


def gate_grad_kernel(place, d_hidden_ref, *refs):
    pieces, weights, (d_gate, d_up, lanes) = refs[:4], refs[4:6], refs[6:]
    gate, up = rows_times(pieces, weights, place[0])
    d_hidden = d_hidden_ref[...]
    sig = jax.nn.sigmoid(gate)
    active = gate * sig
    hidden = (active * up).astype(jnp.bfloat16).astype(jnp.float32)
    dots = jnp.sum(hidden * d_hidden, axis=1, keepdims=True)
    d_gate[...] = (d_hidden * up * sig * (1.0 + gate * (1.0 - sig))).astype(jnp.bfloat16)
    d_up[...] = (d_hidden * active).astype(jnp.bfloat16)
    lane = lax.broadcasted_iota(jnp.int32, lanes.shape, 1)
    lanes[...] = jnp.where(lane == place[1], dots, 0.0).astype(jnp.bfloat16)


def halves_kernel(count, extra, place, *refs):
    lefts, weights, refs = refs[:count], refs[count : 2 * count], refs[2 * count :]
    outs = refs[1:] if extra else refs
    core = place[0]
    half = weights[0].shape[1] // 2
    rows = lefts[0].shape[0] // 2
    for side, mine, pair in ((1 - core, outs[0], outs[1]), (core, outs[2], outs[3])):
        for part in steps_of(half):
            at = pl.ds(pl.multiple_of(side * half + part.start, LANES), part.stop - part.start)
            out = 0.0
            for left, w in zip(lefts, weights):
                out = out + jnp.dot(left[...], w[:, at], preferred_element_type=jnp.float32)
            out = out.astype(jnp.bfloat16)
            mine[:, part] = out[:rows]
            pair[:, part] = out[rows:]
        if extra:
            mine[:, half:] = refs[0][:rows]
            pair[:, half:] = refs[0][rows:]


def halves(place, lefts, weights, more=()):
    rows, units = lefts[0].shape
    width = weights[0].shape[1]
    extra = sum(m.shape[1] for m in more)
    out = vmem((rows // 2, width // 2 + extra), jnp.bfloat16)
    args = (place, *lefts, *weights, *more)
    outs = call(
        functools.partial(halves_kernel, len(lefts), extra),
        (out,) * 4,
        [PLACE] + [HERE] * (len(args) - 1),
        [],
        2 * rows * width * units * len(lefts),
        2 * width * (rows + units * len(lefts)),
        args,
    )
    return outs[:2], outs[2:]


def expert_forward(place, pieces, gate_w, up_w, down_w):
    width, units = gate_w.shape
    rows = 4 * PIECE
    hidden = call(
        hidden_kernel,
        vmem((rows, units), jnp.bfloat16),
        [PLACE] + [HERE] * 6,
        [],
        4 * rows * width * units,
        2 * width * (rows + 2 * units),
        (place, *pieces, gate_w, up_w),
    )
    return halves(place, [hidden], [down_w])


def expert_backward(place, x_pieces, y_pieces, gate_w, up_w, down_t, gate_t, up_t):
    width, units = gate_w.shape
    rows = 4 * PIECE
    d_hidden = call(
        hidden_grad_kernel,
        vmem((rows, units), jnp.float32),
        [PLACE] + [HERE] * 5,
        [],
        2 * rows * width * units,
        2 * width * (rows + units),
        (place, *y_pieces, down_t),
    )
    narrow = vmem((rows, units), jnp.bfloat16)
    d_gate, d_up, lanes = call(
        gate_grad_kernel,
        (narrow, narrow, vmem((rows, LANES), jnp.bfloat16)),
        [PLACE] + [HERE] * 7,
        [],
        4 * rows * width * units,
        2 * width * (rows + 2 * units),
        (place, d_hidden, *x_pieces, gate_w, up_w),
    )
    return halves(place, [d_gate, d_up], [gate_t, up_t], (lanes,))


def mix_kernel(first_choice, extra, place, slots, values, rows, keep, give):
    tokens = slots.shape[0]
    chosen = range(first_choice, first_choice + TOPK)
    half = give.shape[1]
    column = lax.broadcasted_iota(jnp.int32, (tokens, rows.shape[0]), 1)
    hits = [slots[:, k : k + 1] == column for k in chosen]
    weight = 0.0
    for k, hit in zip(chosen, hits):
        weight = weight + jnp.where(hit, values[:, k : k + 1], 0.0)
    parts = []
    for _ in range(3):
        parts.append(weight.astype(jnp.bfloat16))
        weight = weight - parts[-1].astype(jnp.float32)
    weight = jnp.concatenate(parts)
    core = place[0]
    count = tokens // SOURCES

    def split(total):
        first = jnp.concatenate([total[:count], total[2 * count : 3 * count]])
        second = jnp.concatenate([total[count : 2 * count], total[3 * count :]])
        return jnp.where(core == 0, first, second), jnp.where(core == 0, second, first)

    for part in steps_of(half):
        total = jnp.dot(weight, rows[:, part], preferred_element_type=jnp.float32)
        total = total[:tokens] + total[tokens : 2 * tokens] + total[2 * tokens :]
        mine, other = split(total)
        keep[:, part] = mine
        give[:, part] = other.astype(jnp.bfloat16)
    if extra:
        lane = lax.broadcasted_iota(jnp.int32, (tokens, LANES), 1)
        total = 0.0
        for k, hit in enumerate(hits):
            dots = jnp.dot(
                hit.astype(jnp.float32).astype(jnp.bfloat16),
                rows[:, half:],
                preferred_element_type=jnp.float32,
            )
            total = total + jnp.where(lane == k, jnp.sum(dots, axis=1, keepdims=True), 0.0)
        keep[:, half:] = split(total)[0]


def mixed(place, slots, values, first_choice, rows, extra, core):
    tokens = slots.shape[0]
    half = rows.shape[1] - extra
    keep, give = call(
        functools.partial(mix_kernel, first_choice, extra),
        (
            jax.ShapeDtypeStruct((tokens // 2, half + extra), jnp.float32),
            jax.ShapeDtypeStruct((tokens // 2, half), jnp.bfloat16),
        ),
        [PLACE] + [HERE] * 3,
        [],
        6 * tokens * 2 * PIECE * half,
        2 * 2 * PIECE * half,
        (place, slots, values, rows),
    )
    got = send(give, SWAP_CORE).astype(jnp.float32)
    kept = keep[:, :half]
    whole = jnp.where(
        core == 0,
        jnp.concatenate([kept, got], axis=1),
        jnp.concatenate([got, kept], axis=1),
    )
    count = tokens // SOURCES
    if extra:
        whole = jnp.concatenate([whole, keep[:, half:]], axis=1)
    return whole[:count], whole[count:].astype(jnp.bfloat16)


def local(
    act_fwd, act_saved, cot_in, routes_fwd, routes_bwd, w_gate, w_up, w_down, router, norm_gain
):
    gate_cols = w_gate[0]
    up_cols = w_up[0]
    down_rows = w_down[0]
    table = router[0]
    gain = norm_gain[0]
    fwd_rows = act_fwd[0]
    saved_rows = act_saved[0]
    grad_in = cot_in[0]
    index = lax.axis_index("ep")
    y, z, core = place_of(index)
    place = jnp.stack([core, index % 4, y, z]).astype(jnp.int32)

    ids = jnp.concatenate([routes_bwd[0], routes_fwd[0]], axis=1)
    grad_mine = share_cores(grad_in, core, ids)
    grad_other = send(grad_mine, SWAP_Y)
    normed_bwd, inverse_bwd = normalize(saved_rows, gain)
    bwd_mine = share_cores(normed_bwd, core)
    grad_kept, grad_near, slots = pack(
        place, 0, (grad_mine, after(grad_other, bwd_mine)), task="ids"
    )
    bwd_mine = after(bwd_mine, grad_near)
    bwd_other = send(bwd_mine, SWAP_Y)

    grad_entered = enter(grad_kept, grad_near)
    bwd_kept, bwd_near = pack(place, 0, (bwd_mine, after(bwd_other, grad_entered[1])), slots)

    normed_fwd, _ = normalize(after(fwd_rows, bwd_near), gain)
    weights_bwd, chosen, summed, onehot = gate_values(
        after(normed_bwd, bwd_near), table, routes_bwd[0]
    )
    weights_fwd = gate_values(normed_fwd, table, routes_fwd[0])[0]
    weights = three_parts(jnp.concatenate([weights_bwd, weights_fwd], axis=1))
    fwd_mine = share_cores(normed_fwd, core, weights)
    fwd_other = send(fwd_mine, SWAP_Y)

    *grad_chip, grad_far = spread(*grad_entered, (fwd_mine,))
    bwd_entered = enter(bwd_kept, bwd_near, (grad_far,))
    fwd_kept, fwd_near, values = pack(
        place, TOPK, (fwd_mine, after(fwd_other, bwd_entered[1])), slots, task="values"
    )
    gate_t = turn(after(gate_cols, fwd_near))
    up_t = turn(after(up_cols, fwd_near))
    down_t = turn(after(down_rows, fwd_near))
    fwd_entered = enter(fwd_kept, fwd_near)
    bwd_chip, bwd_pair, _ = spread(*bwd_entered, fwd_entered + (gate_t, up_t, down_t))
    fwd_rows_next = from_behind(after(fwd_rows, fwd_near), "section", 1)
    tables_next = jnp.concatenate([slots.astype(jnp.float32), values], axis=1)
    tables_next = from_behind(tables_next, "section", 1)
    fwd_chip, fwd_pair, _ = spread(*fwd_entered, (fwd_rows_next, tables_next), True)
    bwd_pair = after(bwd_pair, fwd_chip)

    shares = expert_backward(
        place, both_halves(bwd_chip, bwd_pair), both_halves(*grad_chip), gate_cols, up_cols, down_t, gate_t, up_t
    )
    give, keep = shares
    fwd_pair = after(fwd_pair, give[0])
    give = [after(g, fwd_pair) for g in give]
    bwd_pair = send(for_pair(give, keep), SWAP_PAIR)
    bwd_rows = add(keep[0], send(give[0], SWAP_CORE), bwd_pair)
    back_bwd = give_back(bwd_rows)
    pieces = both_halves(fwd_chip, fwd_pair)
    give, keep = expert_forward(place, pieces, gate_cols, up_cols, down_rows)
    give = [after(g, bwd_rows) for g in give]
    fwd_pair = send(for_pair(give, keep), SWAP_PAIR)
    fwd_rows = add(keep[0], send(give[0], SWAP_CORE), fwd_pair)
    back_fwd = give_back_onward(fwd_rows)
    back_bwd = after(back_bwd, fwd_rows)

    near, far = mixed(place, slots, values, 0, back_bwd, LANES, core)
    grad_normed = near + send(far, SWAP_Y).astype(jnp.float32)
    dot_assign = grad_normed[:, -LANES:][:, :TOPK]
    grad_normed = grad_normed[:, :-LANES]
    cross = jnp.sum(dot_assign * chosen, axis=-1, keepdims=True)
    grad_aff = routed_scale * (dot_assign / summed - cross / (summed * summed))
    grad_logit = grad_aff * chosen * (1.0 - chosen)
    grad_table = jnp.sum(onehot * grad_logit[:, :, None], axis=1)
    grad_normed = grad_normed + lax.dot_general(
        grad_table, table, (((1,), (1,)), ((), ())), precision=lax.Precision.HIGHEST
    )
    scaled = gain * grad_normed
    widened = saved_rows.astype(jnp.float32)
    grad_input = (
        inverse_bwd * scaled
        - widened
        * inverse_bwd
        * inverse_bwd
        * inverse_bwd
        * jnp.mean(widened * scaled, axis=-1, keepdims=True)
    )
    result_bwd = (grad_in.astype(jnp.float32) + grad_input).astype(jnp.bfloat16)

    cot_next = from_behind(result_bwd[None], "section", -1)

    slots_next = tables_next[:, : 2 * TOPK].astype(jnp.int32)
    values_next = tables_next[:, 2 * TOPK :]
    near, far = mixed(place, slots_next, values_next, TOPK, back_fwd, 0, core)
    expert_out = near + send(far, SWAP_Y).astype(jnp.float32)
    fwd_next = (fwd_rows_next.astype(jnp.float32) + expert_out).astype(jnp.bfloat16)[None]
    return (fwd_next, cot_next)


def solution(mesh):
    return jax.shard_map(
        local,
        mesh=mesh,
        in_specs=(
            P("section", "ep", None),
            P("section", "ep", None),
            P("section", "ep", None),
            P("section", "ep", None),
            P("section", "ep", None),
            P("section", None, "ep"),
            P("section", None, "ep"),
            P("section", "ep", None),
            P("section", None, None),
            P("section", None),
        ),
        out_specs=(P("section", "ep", None), P("section", "ep", None)),
        check_vma=False,
    )
```

```python
import functools

import jax
import jax.numpy as jnp
from jax import lax
from jax.experimental import pallas as pl
from jax.experimental.pallas import tpu as pltpu
from jax.sharding import PartitionSpec as P

TOPK = 2
CAP = 6
PAIRS = 4
SOURCES = 4
UNIT = SOURCES * CAP
PIECE = 2 * UNIT
LANES = 128
VMEM_LIMIT = 16 * 1024 * 1024

routed_scale = 2.5


def place_of(index):
    return index // 16, index // 2 % 8, index % 2


def route_of(step):
    def target(index):
        y, z, core = place_of(index)
        sign = -1 if z % 2 else 1
        y, z, core = step(y, z, core, sign)
        return y * 16 + z % 8 * 2 + core

    return [(i, target(i)) for i in range(32)]


def back_of(route):
    return [(b, a) for a, b in route]


SWAP_Y = route_of(lambda y, z, core, sign: (1 - y, z, core))
SWAP_CORE = route_of(lambda y, z, core, sign: (y, z, 1 - core))
SWAP_PAIR = route_of(lambda y, z, core, sign: (y, z + sign, core))
NEAR = route_of(lambda y, z, core, sign: (y, z - sign, core))
FAR = route_of(lambda y, z, core, sign: (y, z + 2 * sign, core))
NEAR_FAR = route_of(lambda y, z, core, sign: (y, z - 3 * sign, core))


def send(block, route):
    return lax.ppermute(block, "ep", route)


def after(block, *earlier):
    return lax.optimization_barrier((block,) + earlier)[0]


def from_behind(block, axis, distance):
    devices = range(lax.axis_size(axis))
    route = [((i - distance) % len(devices), i) for i in devices]
    return lax.ppermute(block, axis, route)


def normalize(activations, gain):
    widened = activations.astype(jnp.float32)
    inverse = lax.rsqrt(jnp.mean(widened * widened, axis=-1, keepdims=True) + 1e-06)
    return ((widened * inverse * gain).astype(jnp.bfloat16), inverse)


def gate_values(normed, table, expert_ids):
    logits = jnp.dot(normed.astype(jnp.float32), table, precision=lax.Precision.HIGHEST)
    affinity = jax.nn.sigmoid(logits)
    onehot = (
        expert_ids[:, :, None] == jnp.arange(table.shape[1], dtype=jnp.int32)[None, None, :]
    ).astype(jnp.float32)
    chosen = jnp.sum(onehot * affinity[:, None, :], axis=-1)
    summed = jnp.sum(chosen, axis=-1, keepdims=True)
    return (routed_scale * chosen / summed, chosen, summed, onehot)


def in_core_order(mine, other, core):
    return jnp.where(core == 0, jnp.concatenate([mine, other]), jnp.concatenate([other, mine]))


def half_of(rows, which):
    half = rows.shape[1] // 2
    return lax.dynamic_slice_in_dim(rows, which * half, half, axis=1)


def share_cores(rows, core, lanes=None):
    parts = [half_of(rows, core), half_of(rows, 1 - core)]
    if lanes is not None:
        lanes = jnp.pad(lanes.astype(jnp.bfloat16), ((0, 0), (0, LANES - lanes.shape[1])))
        parts = [jnp.concatenate([p, lanes], axis=1) for p in parts]
    return in_core_order(parts[0], send(parts[1], SWAP_CORE), core)


def three_parts(values):
    first = lax.reduce_precision(values, 8, 7)
    second = lax.reduce_precision(values - first, 8, 7)
    return jnp.concatenate([first, second, values - first - second], axis=1)


def enter(kept, near, wait=()):
    came = after(send(near, NEAR), *wait)
    mine = jnp.concatenate([kept[:UNIT], came[:UNIT]])
    return mine, jnp.concatenate([kept[UNIT:], came[UNIT:]])


def spread(mine, onward, far_wait=(), whole=False):
    far = after(send(onward, FAR), *far_wait)
    chip = jnp.concatenate([mine, far])
    if whole:
        return chip, send(chip, SWAP_PAIR), far
    return chip, jnp.concatenate([send(mine, SWAP_PAIR), send(far, SWAP_PAIR)]), far


def both_halves(chip, pair):
    return [chip, pair, send(chip, SWAP_CORE), send(pair, SWAP_CORE)]


def add(*terms):
    return sum(t.astype(jnp.float32) for t in terms).astype(jnp.bfloat16)


def for_pair(give, keep):
    return add(keep[1], send(give[1], SWAP_CORE))


HOME = [[(i, i) for i in range(32)]] + [back_of(route) for route in (FAR, NEAR, NEAR_FAR)]


def give_back(rows):
    kept, near, far, near_far = jnp.split(rows, PAIRS)
    units = [kept, send(far, HOME[1]), send(near, HOME[2]), send(near_far, HOME[3])]
    return jnp.concatenate(units)


def give_back_onward(rows):
    sections = lax.axis_size("section")
    kept, near, far, near_far = jnp.split(rows, PAIRS)
    units = []
    for unit, route in zip((kept, far, near, near_far), HOME):
        onward = [
            (s * 32 + a, (s + 1) % sections * 32 + b) for s in range(sections) for a, b in route
        ]
        units.append(lax.ppermute(unit, ("section", "ep"), onward))
    return jnp.concatenate(units)


PLACE = pl.BlockSpec(memory_space=pltpu.SMEM)
HERE = pl.BlockSpec(memory_space=pltpu.VMEM)
THERE = pl.BlockSpec(memory_space=pl.ANY)
STEP = 512


def here(array):
    return pltpu.with_memory_space_constraint(array, pltpu.VMEM)


def vmem(shape, dtype):
    return pltpu.VMEM(shape, dtype)


def call(kernel, out_shape, in_specs, scratch_shapes, flops, moved, args):
    args = [here(x) if spec is HERE else x for x, spec in zip(args, in_specs)]
    return pl.pallas_call(
        kernel,
        out_shape=out_shape,
        in_specs=in_specs,
        out_specs=jax.tree.map(lambda _: HERE, out_shape),
        scratch_shapes=scratch_shapes,
        compiler_params=pltpu.CompilerParams(vmem_limit_bytes=VMEM_LIMIT),
        cost_estimate=pl.CostEstimate(flops=flops, bytes_accessed=moved, transcendentals=0),
    )(*args)


def steps_of(size):
    step = STEP if size % STEP == 0 else size
    return [slice(at, at + step) for at in range(0, size, step)]


def slots_of(ids, place):
    y, z = place[2], place[3]
    count = ids[0].shape[0]
    tokens = count // SOURCES
    expert = lax.broadcasted_iota(jnp.int32, (count, LANES), 1)
    onehots = [(i == expert).astype(jnp.float32) for i in ids]
    row = lax.broadcasted_iota(jnp.int32, (count, count), 0)
    column = lax.broadcasted_iota(jnp.int32, (count, count), 1)
    earlier = (column < row) & (column // tokens == row // tokens)
    before = jnp.dot(
        earlier.astype(jnp.float32).astype(jnp.bfloat16),
        sum(onehots).astype(jnp.bfloat16),
        preferred_element_type=jnp.float32,
    )
    source = lax.broadcasted_iota(jnp.int32, (count, 1), 0) // tokens
    slots = []
    for i, onehot in zip(ids, onehots):
        slot = jnp.sum(onehot * before, axis=1, keepdims=True).astype(jnp.int32)
        away = (i + (2 * PAIRS - z // 2)) % PAIRS
        role = jnp.where(z % 2 == 1, (PAIRS - away) % PAIRS, away)
        unit = jnp.where(role == 2, 3, jnp.where(role == 3, 2, role))
        slots.append(jnp.where(i // PAIRS == y, unit * UNIT + source * CAP + slot, -1))
    return slots


def pack_kernel(first, task, place, slots_ref, mine, other, *outs):
    kept, near = outs[:2]
    half = kept.shape[1]
    slots = None
    if task:
        lanes = jnp.concatenate([mine[:, half:], other[:, half:]]).astype(jnp.float32)
    if task == "ids":
        ids = lanes.astype(jnp.int32)
        columns = [ids[:, k : k + 1] for k in range(2 * TOPK)]
        slots = slots_of(columns[:TOPK], place) + slots_of(columns[TOPK:], place)
        for k, slot in enumerate(slots):
            outs[2][:, k : k + 1] = slot
    else:
        slots = [slots_ref[:, k : k + 1] for k in range(2 * TOPK)]
    if task == "values":
        count = 2 * TOPK
        outs[2][...] = lanes[:, :count] + lanes[:, count : 2 * count] + lanes[:, 2 * count : 3 * count]
    tokens = slots[0].shape[0]
    row = lax.broadcasted_iota(jnp.int32, (tokens, LANES), 1)
    hit = (slots[first] == row) | (slots[first + 1] == row)
    placer = hit.astype(jnp.float32).T.astype(jnp.bfloat16)
    for part in steps_of(half):
        rows = jnp.concatenate([mine[:, part], other[:, part]])
        out = jnp.dot(placer, rows, preferred_element_type=jnp.float32).astype(jnp.bfloat16)
        kept[:, part] = out[:PIECE]
        near[:, part] = out[PIECE : 2 * PIECE]


def pack(place, first, tokens, slots=None, task=None):
    mine, other = tokens
    half = mine.shape[1] - (LANES if task else 0)
    count = 2 * mine.shape[0]
    piece = vmem((PIECE, half), jnp.bfloat16)
    outs = (piece, piece)
    if task == "ids":
        outs += (jax.ShapeDtypeStruct((count, 2 * TOPK), jnp.int32),)
        slots = place.reshape(1, -1)
    elif task == "values":
        outs += (jax.ShapeDtypeStruct((count, 2 * TOPK), jnp.float32),)
    return call(
        functools.partial(pack_kernel, first, task),
        outs,
        [PLACE] + [HERE] * 3,
        [],
        2 * LANES * count * half,
        2 * half * (count + 2 * PIECE),
        (place, slots, mine, other),
    )


def turn_kernel(weight, turned):
    for part in steps_of(max(weight.shape)):
        if weight.shape[0] > weight.shape[1]:
            turned[:, part] = weight[part].T
        else:
            turned[part] = weight[:, part].T


def turn(weight):
    return call(
        turn_kernel, vmem(weight.shape[::-1], weight.dtype), [HERE], [], 0, 0, (weight,)
    )


def slots_of(ids, place):
    y, z = place[2], place[3]
    count = ids[0].shape[0]
    tokens = count // SOURCES
    expert = lax.broadcasted_iota(jnp.int32, (count, LANES), 1)
    onehots = [(i == expert).astype(jnp.float32) for i in ids]
    row = lax.broadcasted_iota(jnp.int32, (count, count), 0)
    column = lax.broadcasted_iota(jnp.int32, (count, count), 1)
    earlier = (column < row) & (column // tokens == row // tokens)
    before = jnp.dot(
        earlier.astype(jnp.float32).astype(jnp.bfloat16),
        sum(onehots).astype(jnp.bfloat16),
        preferred_element_type=jnp.float32,
    )
    source = lax.broadcasted_iota(jnp.int32, (count, 1), 0) // tokens
    slots = []
    for i, onehot in zip(ids, onehots):
        slot = jnp.sum(onehot * before, axis=1, keepdims=True).astype(jnp.int32)
        away = (i + (2 * PAIRS - z // 2)) % PAIRS
        role = jnp.where(z % 2 == 1, (PAIRS - away) % PAIRS, away)
        unit = jnp.where(role == 2, 3, jnp.where(role == 3, 2, role))
        slots.append(jnp.where(i // PAIRS == y, unit * UNIT + source * CAP + slot, -1))
    return slots


def pack_kernel(first, task, place, slots_ref, mine, other, *outs):
    kept, near = outs[:2]
    half = kept.shape[1]
    slots = None
    if task:
        lanes = jnp.concatenate([mine[:, half:], other[:, half:]]).astype(jnp.float32)
    if task == "ids":
        ids = lanes.astype(jnp.int32)
        columns = [ids[:, k : k + 1] for k in range(2 * TOPK)]
        slots = slots_of(columns[:TOPK], place) + slots_of(columns[TOPK:], place)
        for k, slot in enumerate(slots):
            outs[2][:, k : k + 1] = slot
    else:
        slots = [slots_ref[:, k : k + 1] for k in range(2 * TOPK)]
    if task == "values":
        count = 2 * TOPK
        outs[2][...] = lanes[:, :count] + lanes[:, count : 2 * count] + lanes[:, 2 * count : 3 * count]
    tokens = slots[0].shape[0]
    row = lax.broadcasted_iota(jnp.int32, (tokens, LANES), 1)
    hit = (slots[first] == row) | (slots[first + 1] == row)
    placer = hit.astype(jnp.float32).T.astype(jnp.bfloat16)
    for part in steps_of(half):
        rows = jnp.concatenate([mine[:, part], other[:, part]])
        out = jnp.dot(placer, rows, preferred_element_type=jnp.float32).astype(jnp.bfloat16)
        kept[:, part] = out[:PIECE]
        near[:, part] = out[PIECE : 2 * PIECE]


def pack(place, first, tokens, slots=None, task=None):
    mine, other = tokens
    half = mine.shape[1] - (LANES if task else 0)
    count = 2 * mine.shape[0]
    piece = vmem((PIECE, half), jnp.bfloat16)
    outs = (piece, piece)
    if task == "ids":
        outs += (jax.ShapeDtypeStruct((count, 2 * TOPK), jnp.int32),)
        slots = place.reshape(1, -1)
    elif task == "values":
        outs += (jax.ShapeDtypeStruct((count, 2 * TOPK), jnp.float32),)
    return call(
        functools.partial(pack_kernel, first, task),
        outs,
        [PLACE] + [HERE] * 3,
        [],
        2 * LANES * count * half,
        2 * half * (count + 2 * PIECE),
        (place, slots, mine, other),
    )


def load_kernel(axis, source, kept, turned, sems):
    parts = steps_of(source.shape[axis])
    copies = []
    for i, part in enumerate(parts):
        at = (slice(None),) * axis + (pl.ds(part.start, part.stop - part.start),)
        copies.append(pltpu.make_async_copy(source.at[at], kept.at[at], sems.at[i]))
    for c in copies:
        c.start()
    for c, part in zip(copies, parts):
        c.wait()
        if axis == 0:
            turned[:, part] = kept[part].T
        else:
            turned[part] = kept[:, part].T


def load(weight):
    rows, columns = weight.shape
    axis = 0 if rows > columns else 1
    count = len(steps_of(weight.shape[axis]))
    return call(
        functools.partial(load_kernel, axis),
        (vmem((rows, columns), weight.dtype), vmem((columns, rows), weight.dtype)),
        [THERE],
        [pltpu.SemaphoreType.DMA((count,))],
        0,
        6 * rows * columns,
        (pltpu.with_memory_space_constraint(weight, pltpu.HBM),),
    )


def rows_times(pieces, weights, core):
    half = pieces[0].shape[1]
    totals = [0.0] * len(weights)
    for side, both in ((core, pieces[:2]), (1 - core, pieces[2:])):
        rows = jnp.concatenate([p[...] for p in both])
        at = pl.ds(pl.multiple_of(side * half, LANES), half)
        for i, w in enumerate(weights):
            totals[i] = totals[i] + jnp.dot(rows, w[at, :], preferred_element_type=jnp.float32)
    return totals


def hidden_grad_kernel(place, *refs):
    pieces, down_t, out = refs[:4], refs[4], refs[5]
    out[...] = rows_times(pieces, [down_t], place[0])[0]


def hidden_kernel(place, *refs):
    pieces, weights, hidden = refs[:4], refs[4:6], refs[6]
    gate, up = rows_times(pieces, weights, place[0])
    hidden[...] = (gate * jax.nn.sigmoid(gate) * up).astype(jnp.bfloat16)


def gate_grad_kernel(place, d_hidden_ref, *refs):
    pieces, weights, (d_gate, d_up, lanes) = refs[:4], refs[4:6], refs[6:]
    gate, up = rows_times(pieces, weights, place[0])
    d_hidden = d_hidden_ref[...]
    sig = jax.nn.sigmoid(gate)
    active = gate * sig
    hidden = (active * up).astype(jnp.bfloat16).astype(jnp.float32)
    dots = jnp.sum(hidden * d_hidden, axis=1, keepdims=True)
    d_gate[...] = (d_hidden * up * sig * (1.0 + gate * (1.0 - sig))).astype(jnp.bfloat16)
    d_up[...] = (d_hidden * active).astype(jnp.bfloat16)
    lane = lax.broadcasted_iota(jnp.int32, lanes.shape, 1)
    lanes[...] = jnp.where(lane == place[1], dots, 0.0).astype(jnp.bfloat16)


def halves_kernel(count, extra, place, *refs):
    lefts, weights, refs = refs[:count], refs[count : 2 * count], refs[2 * count :]
    outs = refs[1:] if extra else refs
    core = place[0]
    half = weights[0].shape[1] // 2
    rows = lefts[0].shape[0] // 2
    for side, mine, pair in ((1 - core, outs[0], outs[1]), (core, outs[2], outs[3])):
        for part in steps_of(half):
            at = pl.ds(pl.multiple_of(side * half + part.start, LANES), part.stop - part.start)
            out = 0.0
            for left, w in zip(lefts, weights):
                out = out + jnp.dot(left[...], w[:, at], preferred_element_type=jnp.float32)
            out = out.astype(jnp.bfloat16)
            mine[:, part] = out[:rows]
            pair[:, part] = out[rows:]
        if extra:
            mine[:, half:] = refs[0][:rows]
            pair[:, half:] = refs[0][rows:]


def halves(place, lefts, weights, more=()):
    rows, units = lefts[0].shape
    width = weights[0].shape[1]
    extra = sum(m.shape[1] for m in more)
    out = vmem((rows // 2, width // 2 + extra), jnp.bfloat16)
    args = (place, *lefts, *weights, *more)
    outs = call(
        functools.partial(halves_kernel, len(lefts), extra),
        (out,) * 4,
        [PLACE] + [HERE] * (len(args) - 1),
        [],
        2 * rows * width * units * len(lefts),
        2 * width * (rows + units * len(lefts)),
        args,
    )
    return outs[:2], outs[2:]


def expert_forward(place, pieces, gate_w, up_w, down_w):
    width, units = gate_w.shape
    rows = 4 * PIECE
    hidden = call(
        hidden_kernel,
        vmem((rows, units), jnp.bfloat16),
        [PLACE] + [HERE] * 6,
        [],
        4 * rows * width * units,
        2 * width * (rows + 2 * units),
        (place, *pieces, gate_w, up_w),
    )
    return halves(place, [hidden], [down_w])


def expert_backward(place, x_pieces, y_pieces, gate_w, up_w, down_t, gate_t, up_t):
    width, units = gate_w.shape
    rows = 4 * PIECE
    d_hidden = call(
        hidden_grad_kernel,
        vmem((rows, units), jnp.float32),
        [PLACE] + [HERE] * 5,
        [],
        2 * rows * width * units,
        2 * width * (rows + units),
        (place, *y_pieces, down_t),
    )
    narrow = vmem((rows, units), jnp.bfloat16)
    d_gate, d_up, lanes = call(
        gate_grad_kernel,
        (narrow, narrow, vmem((rows, LANES), jnp.bfloat16)),
        [PLACE] + [HERE] * 7,
        [],
        4 * rows * width * units,
        2 * width * (rows + 2 * units),
        (place, d_hidden, *x_pieces, gate_w, up_w),
    )
    return halves(place, [d_gate, d_up], [gate_t, up_t], (lanes,))


def mix_kernel(first_choice, extra, place, slots, values, rows, keep, give):
    tokens = slots.shape[0]
    chosen = range(first_choice, first_choice + TOPK)
    half = give.shape[1]
    column = lax.broadcasted_iota(jnp.int32, (tokens, rows.shape[0]), 1)
    hits = [slots[:, k : k + 1] == column for k in chosen]
    weight = 0.0
    for k, hit in zip(chosen, hits):
        weight = weight + jnp.where(hit, values[:, k : k + 1], 0.0)
    parts = []
    for _ in range(3):
        parts.append(weight.astype(jnp.bfloat16))
        weight = weight - parts[-1].astype(jnp.float32)
    weight = jnp.concatenate(parts)
    core = place[0]
    count = tokens // SOURCES

    def split(total):
        first = jnp.concatenate([total[:count], total[2 * count : 3 * count]])
        second = jnp.concatenate([total[count : 2 * count], total[3 * count :]])
        return jnp.where(core == 0, first, second), jnp.where(core == 0, second, first)

    for part in steps_of(half):
        total = jnp.dot(weight, rows[:, part], preferred_element_type=jnp.float32)
        total = total[:tokens] + total[tokens : 2 * tokens] + total[2 * tokens :]
        mine, other = split(total)
        keep[:, part] = mine
        give[:, part] = other.astype(jnp.bfloat16)
    if extra:
        lane = lax.broadcasted_iota(jnp.int32, (tokens, LANES), 1)
        total = 0.0
        for k, hit in enumerate(hits):
            dots = jnp.dot(
                hit.astype(jnp.float32).astype(jnp.bfloat16),
                rows[:, half:],
                preferred_element_type=jnp.float32,
            )
            total = total + jnp.where(lane == k, jnp.sum(dots, axis=1, keepdims=True), 0.0)
        keep[:, half:] = split(total)[0]


def mixed(place, slots, values, first_choice, rows, extra, core):
    tokens = slots.shape[0]
    half = rows.shape[1] - extra
    keep, give = call(
        functools.partial(mix_kernel, first_choice, extra),
        (
            jax.ShapeDtypeStruct((tokens // 2, half + extra), jnp.float32),
            jax.ShapeDtypeStruct((tokens // 2, half), jnp.bfloat16),
        ),
        [PLACE] + [HERE] * 3,
        [],
        6 * tokens * 2 * PIECE * half,
        2 * 2 * PIECE * half,
        (place, slots, values, rows),
    )
    got = send(give, SWAP_CORE).astype(jnp.float32)
    kept = keep[:, :half]
    whole = jnp.where(
        core == 0,
        jnp.concatenate([kept, got], axis=1),
        jnp.concatenate([got, kept], axis=1),
    )
    count = tokens // SOURCES
    if extra:
        whole = jnp.concatenate([whole, keep[:, half:]], axis=1)
    return whole[:count], whole[count:].astype(jnp.bfloat16)


def local(
    act_fwd, act_saved, cot_in, routes_fwd, routes_bwd, w_gate, w_up, w_down, router, norm_gain
):
    gate_cols = w_gate[0]
    up_cols = w_up[0]
    down_rows = w_down[0]
    table = router[0]
    gain = norm_gain[0]
    fwd_rows = act_fwd[0]
    saved_rows = act_saved[0]
    grad_in = cot_in[0]
    index = lax.axis_index("ep")
    y, z, core = place_of(index)
    place = jnp.stack([core, index % 4, y, z]).astype(jnp.int32)

    ids = jnp.concatenate([routes_bwd[0], routes_fwd[0]], axis=1)
    grad_mine = share_cores(grad_in, core, ids)
    grad_other = send(grad_mine, SWAP_Y)
    normed_bwd, inverse_bwd = normalize(saved_rows, gain)
    bwd_mine = share_cores(normed_bwd, core)
    grad_kept, grad_near, slots = pack(
        place, 0, (grad_mine, after(grad_other, bwd_mine)), task="ids"
    )
    bwd_mine = after(bwd_mine, grad_near)
    bwd_other = send(bwd_mine, SWAP_Y)

    grad_entered = enter(grad_kept, grad_near)
    bwd_kept, bwd_near = pack(place, 0, (bwd_mine, after(bwd_other, grad_entered[1])), slots)

    normed_fwd, _ = normalize(after(fwd_rows, bwd_near), gain)
    weights_bwd, chosen, summed, onehot = gate_values(
        after(normed_bwd, bwd_near), table, routes_bwd[0]
    )
    weights_fwd = gate_values(normed_fwd, table, routes_fwd[0])[0]
    weights = three_parts(jnp.concatenate([weights_bwd, weights_fwd], axis=1))
    fwd_mine = share_cores(normed_fwd, core, weights)
    fwd_other = send(fwd_mine, SWAP_Y)

    *grad_chip, grad_far = spread(*grad_entered, (fwd_mine,))
    bwd_entered = enter(bwd_kept, bwd_near, (grad_far,))
    fwd_kept, fwd_near, values = pack(
        place, TOPK, (fwd_mine, after(fwd_other, bwd_entered[1])), slots, task="values"
    )
    gate_t = turn(after(gate_cols, fwd_near))
    up_t = turn(after(up_cols, fwd_near))
    down_t = turn(after(down_rows, fwd_near))
    fwd_entered = enter(fwd_kept, fwd_near)
    bwd_chip, bwd_pair, _ = spread(*bwd_entered, fwd_entered + (gate_t, up_t, down_t))
    fwd_rows_next = from_behind(after(fwd_rows, fwd_near), "section", 1)
    tables_next = jnp.concatenate([slots.astype(jnp.float32), values], axis=1)
    tables_next = from_behind(tables_next, "section", 1)
    fwd_chip, fwd_pair, _ = spread(*fwd_entered, (fwd_rows_next, tables_next), True)
    bwd_pair = after(bwd_pair, fwd_chip)

    shares = expert_backward(
        place, both_halves(bwd_chip, bwd_pair), both_halves(*grad_chip), gate_cols, up_cols, down_t, gate_t, up_t
    )
    give, keep = shares
    fwd_pair = after(fwd_pair, give[0])
    give = [after(g, fwd_pair) for g in give]
    bwd_pair = send(for_pair(give, keep), SWAP_PAIR)
    bwd_rows = add(keep[0], send(give[0], SWAP_CORE), bwd_pair)
    back_bwd = give_back(bwd_rows)
    pieces = both_halves(fwd_chip, fwd_pair)
    give, keep = expert_forward(place, pieces, gate_cols, up_cols, down_rows)
    fwd_pair = after(send(for_pair(give, keep), SWAP_PAIR), bwd_rows)
    fwd_rows = add(keep[0], send(give[0], SWAP_CORE), fwd_pair)
    back_fwd = give_back_onward(fwd_rows)
    back_bwd = after(back_bwd, fwd_rows)

    near, far = mixed(place, slots, values, 0, back_bwd, LANES, core)
    grad_normed = near + send(far, SWAP_Y).astype(jnp.float32)
    dot_assign = grad_normed[:, -LANES:][:, :TOPK]
    grad_normed = grad_normed[:, :-LANES]
    cross = jnp.sum(dot_assign * chosen, axis=-1, keepdims=True)
    grad_aff = routed_scale * (dot_assign / summed - cross / (summed * summed))
    grad_logit = grad_aff * chosen * (1.0 - chosen)
    grad_table = jnp.sum(onehot * grad_logit[:, :, None], axis=1)
    grad_normed = grad_normed + lax.dot_general(
        grad_table, table, (((1,), (1,)), ((), ())), precision=lax.Precision.HIGHEST
    )
    scaled = gain * grad_normed
    widened = saved_rows.astype(jnp.float32)
    grad_input = (
        inverse_bwd * scaled
        - widened
        * inverse_bwd
        * inverse_bwd
        * inverse_bwd
        * jnp.mean(widened * scaled, axis=-1, keepdims=True)
    )
    result_bwd = (grad_in.astype(jnp.float32) + grad_input).astype(jnp.bfloat16)

    cot_next = from_behind(result_bwd[None], "section", -1)

    slots_next = tables_next[:, : 2 * TOPK].astype(jnp.int32)
    values_next = tables_next[:, 2 * TOPK :]
    near, far = mixed(place, slots_next, values_next, TOPK, back_fwd, 0, core)
    expert_out = near + send(far, SWAP_Y).astype(jnp.float32)
    fwd_next = (fwd_rows_next.astype(jnp.float32) + expert_out).astype(jnp.bfloat16)[None]
    return (fwd_next, cot_next)


def solution(mesh):
    return jax.shard_map(
        local,
        mesh=mesh,
        in_specs=(
            P("section", "ep", None),
            P("section", "ep", None),
            P("section", "ep", None),
            P("section", "ep", None),
            P("section", "ep", None),
            P("section", None, "ep"),
            P("section", None, "ep"),
            P("section", "ep", None),
            P("section", None, None),
            P("section", None),
        ),
        out_specs=(P("section", "ep", None), P("section", "ep", None)),
        check_vma=False,
    )
```
